256 devices in a mesh: leaf: 64 (over z, y, x_hi), row: 4 (over x_lo, core).
Axes of the slice: x: 4 (x_hi: 2, x_lo: 2; x = x_hi * 2 + x_lo), y: 4, z: 8, core: 2. Of those that a mesh axis runs over, the one named last changes fastest.
Arguments:
- coords: float32 [3, 65536], P(None, ('leaf', 'row')), may hold values from 0 to 1
- order: int32 [65536], P(('leaf', 'row')), may hold values from 0 to 65535, each once
- targets: float32 [65536, 128], P(('leaf', 'row')), may hold values from -6 to 6
- bases: float32 [6, 65536, 128], P(None, ('leaf', 'row')), may hold values from -1 to 1
Outputs:
- solution: float32 [65536, 128], P(('leaf', 'row'))
The draws below stay inside these ranges and needn't reach their ends.
Inputs may be any that keep to these rules, and one draw needn't show every extreme that they name: order holds every number below 65536 once.
All inputs are finite; a program needn't handle non-finite values.
Results may differ from the reference program's by a relative error of at most 0.00022.
Values sent between devices are 32-bit elements; how exact they have to be, the bound alone decides.
No kernel may reach another device: no remote copies, remote signals or barrier semaphores. Data moves between devices by JAX's collectives and lax.ppermute only.
A program may use at most 128 MiB of HBM per device.

```python
import jax
import jax.numpy as jnp
from jax import lax

LEAF = 1024
RANK = 128
NRHS = 128
LEVELS = 6
POINTS = 65536
N_LEAF = 64


def steps_of(key, shape, cuts, least, high):
    factor_of = 1.0
    for axis_at, shards_of in cuts:
        steps = jax.random.uniform(jax.random.fold_in(jax.random.fold_in(key, 6), axis_at), (shards_of,), jnp.float32, least / len(cuts), high / len(cuts))
        factor_of = factor_of * jnp.repeat(jnp.exp(steps), shape[axis_at] // shards_of).reshape((-1,) + (1,) * (len(shape) - 1 - axis_at))
    return factor_of


def bell_draw(rng, shape, width, reach, cuts=(), kind=jnp.bfloat16):
    loudness = steps_of(rng, shape, cuts, -0.22, 0.18) if cuts else 1.0
    values = jax.random.normal(rng, shape, jnp.float32) * width * loudness
    return jnp.minimum(jnp.maximum(values, -reach), reach).astype(kind)


def setup_inputs(seed: int = 0) -> dict:
    seeds = jax.random.split(jax.random.key(seed), 5)
    return {
        "coords": jnp.clip(1.0 * jax.random.uniform(seeds[0], (3, POINTS), jnp.float32) ** steps_of(seeds[0], (3, POINTS), ((1, 256),), -0.2, 0.2), 0.0, 1.0),
        "order": jax.random.permutation(seeds[1], POINTS).astype(jnp.int32),
        "targets": bell_draw(seeds[2], (POINTS, NRHS), 1.0, 6.0, ((0, 256),), jnp.float32),
        "bases": jnp.clip(jax.random.uniform(seeds[3], (LEVELS, POINTS, RANK), jnp.float32, -1.0, 1.0) * steps_of(seeds[3], (LEVELS, POINTS, RANK), ((1, 256),), -0.4, 0.0), -1.0, 1.0),
    }


LENGTH_SCALE = 0.1
NOISE_VAR = 1.0
PRECISE = lax.Precision.HIGHEST

def lower_solve(factor, right):
    return lax.linalg.triangular_solve(factor, right, left_side=True, lower=True)

def upper_solve(factor, right):
    return lax.linalg.triangular_solve(factor, right, left_side=True, lower=True, transpose_a=True)

def chol_solve(factor, right):
    return upper_solve(factor, lower_solve(factor, right))

def leaf_kernel(row_points, col_points, first_row):
    squared = jnp.zeros((row_points.shape[1], col_points.shape[1]), jnp.float32)
    for axis_index in range(3):
        offset = row_points[axis_index][:, None] - col_points[axis_index][None, :]
        squared = squared + offset * offset
    kernel = jnp.exp(squared * (-0.5 / (LENGTH_SCALE * LENGTH_SCALE)))
    row_ids = first_row + jnp.arange(row_points.shape[1], dtype=jnp.int32)
    col_ids = jnp.arange(col_points.shape[1], dtype=jnp.int32)
    return kernel + NOISE_VAR * (row_ids[:, None] == col_ids[None, :]).astype(jnp.float32)

def merge_coeffs(own_sum, sibling, is_left, rank_cols):
    part_a = jnp.where(is_left, own_sum, sibling)
    part_b = jnp.where(is_left, sibling, own_sum)
    gram_a = 0.5 * (part_a[:, :rank_cols] + part_a[:, :rank_cols].T)
    gram_b = 0.5 * (part_b[:, :rank_cols] + part_b[:, :rank_cols].T)
    proj_a = part_a[:, rank_cols:]
    proj_b = part_b[:, rank_cols:]
    identity = jnp.eye(rank_cols, dtype=jnp.float32)
    chol_b = jnp.linalg.cholesky(gram_b)
    inv_b = chol_solve(chol_b, identity)
    middle = 0.5 * (inv_b + inv_b.T) - gram_a
    chol_m = jnp.linalg.cholesky(middle)
    residual = proj_a - jnp.dot(gram_a.astype(jnp.float32), proj_b.astype(jnp.float32), preferred_element_type=jnp.float32, precision=PRECISE)
    weighted = chol_solve(chol_m, residual)
    coef_a = proj_b - weighted
    coef_b = chol_solve(chol_b, weighted)
    return jnp.where(is_left, coef_a, coef_b)

def reference(coords, order, targets, bases):
    points = coords[:, order]
    scaled = [bases[level_index] * float((LEAF * 2 ** level_index) ** (-0.5)) for level_index in range(LEVELS)]
    stacked = jnp.concatenate(scaled + [targets], axis=1)
    total_width = stacked.shape[1]
    leaf_pts = points.reshape(3, N_LEAF, LEAF).transpose(1, 0, 2)
    leaf_rhs = stacked.reshape(N_LEAF, LEAF, total_width)

    def factor_leaf(packed):
        kernel = leaf_kernel(packed[0], packed[0], jnp.int32(0))
        factor = jnp.linalg.cholesky(kernel)
        return (factor, lower_solve(factor, packed[1]))
    factors, whitened = lax.map(factor_leaf, (leaf_pts, leaf_rhs))
    current = whitened
    for level_index in range(LEVELS):
        group_size = 2 ** level_index
        node_count = N_LEAF // (2 * group_size)
        first_col = level_index * RANK
        left_basis = whitened[:, :, first_col:first_col + RANK].reshape(node_count, 2, group_size * LEAF, RANK)
        shaped = current.reshape(node_count, 2, group_size * LEAF, total_width)
        child_sums = jnp.einsum('nsrk,nsrc->nskc', left_basis, shaped[..., first_col:], precision=PRECISE)
        coef_a = jax.vmap(lambda own_sum, sibling: merge_coeffs(own_sum, sibling, True, RANK))(child_sums[:, 0], child_sums[:, 1])
        coef_b = jax.vmap(lambda own_sum, sibling: merge_coeffs(own_sum, sibling, False, RANK))(child_sums[:, 1], child_sums[:, 0])
        both_coefs = jnp.stack([coef_a, coef_b], axis=1)
        update = jnp.einsum('nsrk,nskc->nsrc', shaped[..., first_col:first_col + RANK], both_coefs, precision=PRECISE)
        corrected = shaped[..., first_col + RANK:] - update
        shaped = jnp.concatenate([shaped[..., :first_col + RANK], corrected], axis=-1)
        current = shaped.reshape(N_LEAF, LEAF, total_width)
    answer = current[:, :, LEVELS * RANK:]
    solution = lax.map(lambda packed: upper_solve(packed[0], packed[1]), (factors, answer))
    return solution.reshape(N_LEAF * LEAF, NRHS)
```

```python
import functools

import jax
import jax.numpy as jnp
from jax import lax
from jax.experimental import pallas as pl
from jax.experimental.pallas import tpu as pltpu
from jax.sharding import PartitionSpec as P

LENGTH_SCALE = 0.1
NOISE_VAR = 1.0
BLOCK = 128
ROUNDING = 3e-8
AXES = ("leaf", "row")
F32 = jnp.float32


def params():
    return pltpu.CompilerParams(vmem_limit_bytes=48 * 1024 * 1024)


def swap(value, mask):
    count = lax.axis_size(AXES)
    return lax.ppermute(value, AXES, [(index, index ^ mask) for index in range(count)])


def split(value):
    high = value.astype(jnp.bfloat16)
    return high, (value - high.astype(F32)).astype(jnp.bfloat16)


def full_dot(left, right):
    return jnp.dot(left, right, preferred_element_type=F32, precision=lax.Precision.HIGHEST)


def half_dot(left, right):
    return jnp.dot(left, right, preferred_element_type=F32)


def eye():
    rows = lax.broadcasted_iota(jnp.int32, (BLOCK, BLOCK), 0)
    cols = lax.broadcasted_iota(jnp.int32, (BLOCK, BLOCK), 1)
    return (rows == cols).astype(F32)


def cols(index, count=1):
    return slice(index * BLOCK, (index + count) * BLOCK)


def lookup_kernel(order_ref, table_ref, out_ref):
    mine = lax.axis_index("row")
    numbers = order_ref[...]
    owner = numbers >> 8
    leaves = table_ref.shape[0]
    key = jnp.where((owner & 3) == mine, ((numbers >> 7) & 1) * leaves + (owner >> 2), -1)
    shape = (2 * leaves, numbers.shape[1])
    chosen = (lax.broadcasted_iota(jnp.int32, shape, 0) == key).astype(F32)
    lane = lax.broadcasted_iota(jnp.int32, (BLOCK, numbers.shape[1]), 0) == (numbers & 127)
    out_ref[...] = jnp.zeros_like(out_ref)
    for part in range(3):
        piece = jnp.concatenate([table_ref[:, 2 * part, :], table_ref[:, 2 * part + 1, :]], axis=0)
        found = full_dot(piece.T, chosen)
        out_ref[part : part + 1, :] = jnp.sum(jnp.where(lane, found, 0.0), axis=0, keepdims=True)


def lookup(order_row, table):
    return pl.pallas_call(
        lookup_kernel,
        out_shape=jax.ShapeDtypeStruct((8, order_row.shape[1]), F32),
        compiler_params=params(),
        name="lookup",
    )(order_row, table)


def geometric_inverse(power, steps, bound, held):
    total = eye() + power
    power = full_dot(power, power)
    for step in range(1, steps):
        total = total + full_dot(power, total)
        if step + 1 < steps:
            power = full_dot(power, power)

    held[0], held[1] = power, total

    def once(bound):
        power = full_dot(held[0], held[0])
        held[0] = power
        held[1] += full_dot(power, held[1])
        return bound * bound

    lax.while_loop(lambda bound: bound > ROUNDING, once, bound)
    return held[1]


def pivot_inverse(pivot, held):
    largest = jnp.max(jnp.sum(jnp.abs(pivot), axis=0, keepdims=True), axis=1, keepdims=True)
    scale = 2.0 / (1.0 + largest)
    ratio = (largest - 1.0) / (largest + 1.0)
    for _ in range(6):
        ratio = ratio * ratio
    return scale * geometric_inverse(eye() - scale * pivot, 6, jnp.max(ratio), held)


def leaf_kernel(
    own_ref, core_ref, chip_ref, far_ref, *refs, levels, scales
):
    basis_refs, target_refs = refs[:4], refs[4:8]
    first_ref, first_half_ref, rest_ref, rest_half_ref, own_x_ref = refs[8:13]
    mat_ref, rhs_ref, sol_ref, held_ref = refs[13:17]
    size = mat_ref.shape[0]
    blocks = size // BLOCK
    piece = size // 4
    width = rhs_ref.shape[1]
    core = lax.axis_index("row") & 1
    pieces = []
    for spot in range(4):
        total = own_ref[:, spot * piece : (spot + 1) * piece]
        for mask, ref in ((1, core_ref), (2, chip_ref), (3, far_ref)):
            other = spot ^ mask
            total = total + ref[:, other * piece : (other + 1) * piece]
        pieces.append(total)
    points = jnp.concatenate(pieces, axis=1)
    for spot in range(4):
        rows = slice(spot * piece, (spot + 1) * piece)
        for level in range(levels):
            rhs_ref[rows, cols(level)] = basis_refs[spot][level] * scales[level]
        rhs_ref[rows, cols(levels)] = target_refs[spot][...]
    for block in range(blocks):
        turned = points[:, cols(block)].T
        squared = jnp.zeros((BLOCK, size), F32)
        for part in range(3):
            offset = turned[:, part : part + 1] - points[part : part + 1, :]
            squared = squared + offset * offset
        value = jnp.exp(squared * (-0.5 / (LENGTH_SCALE * LENGTH_SCALE)))
        mat_ref[cols(block), :] = value
        mat_ref[cols(block), cols(block)] = value[:, cols(block)] + NOISE_VAR * eye()
    pivot = mat_ref[cols(0), cols(0)]
    right = None
    for block in range(blocks):
        inverse = pivot_inverse(pivot, held_ref)
        after = blocks - block - 1
        solved = full_dot(inverse, rhs_ref[cols(block), :])
        sol_ref[cols(block), :] = solved
        if after == 0:
            break
        right = full_dot(inverse, mat_ref[cols(block), cols(block + 1, after)])
        down = mat_ref[cols(block + 1, after), cols(block)]
        pivot = mat_ref[cols(block + 1), cols(block + 1)] - full_dot(
            down[:BLOCK], right[:, :BLOCK]
        )
        high, low = split(down)
        left = jnp.concatenate([high, high, low], axis=1)
        high, low = split(right)
        mat_ref[cols(block + 1, after), cols(block + 1, after)] -= half_dot(
            left, jnp.concatenate([high, low, high], axis=0)
        )
        high, low = split(solved)
        rhs_ref[cols(block + 1, after), :] -= half_dot(
            left, jnp.concatenate([high, low, high], axis=0)
        )
    own_x_ref[cols(1), :] = sol_ref[cols(blocks - 1), :]
    own_x_ref[cols(0), :] = sol_ref[cols(blocks - 2), :] - full_dot(
        right, sol_ref[cols(blocks - 1), :]
    )
    high, low = split(sol_ref[...])
    start = 0
    for level in range(levels):
        left_high, left_low = split(rhs_ref[:, cols(level)].T)
        from_here = slice(level * BLOCK, width)
        sums = half_dot(left_high, high[:, from_here]) + (
            half_dot(left_high, low[:, from_here]) + half_dot(left_low, high[:, from_here])
        )
        if level == 0:
            first_ref[...] = sums
        else:
            rest_ref[:, start : start + sums.shape[1]] = sums
            start += sums.shape[1]
    half = pl.ds(pl.multiple_of(core * (BLOCK // 2), BLOCK // 2), BLOCK // 2)
    first_half_ref[...] = first_ref[half, :]
    rest_half_ref[...] = rest_ref[half, :]


def rest_width(level, levels):
    return sum((levels + 1 - row) * BLOCK for row in range(level + 1, levels))


def shape_of(*shape):
    return jax.ShapeDtypeStruct(shape, F32)


def leaf(parts, bases, targets, scales):
    levels = len(scales)
    size = parts[0].shape[1]
    width = (levels + 1) * BLOCK
    rest = rest_width(0, levels)
    return pl.pallas_call(
        functools.partial(leaf_kernel, levels=levels, scales=scales),
        out_shape=[
            shape_of(BLOCK, width),
            shape_of(BLOCK // 2, width),
            shape_of(BLOCK, rest),
            shape_of(BLOCK // 2, rest),
            shape_of(2 * BLOCK, width),
        ],
        scratch_shapes=[
            pltpu.VMEM((size, size), F32),
            pltpu.VMEM((size, width), F32),
            pltpu.VMEM((size, width), F32),
            pltpu.VMEM((2, BLOCK, BLOCK), F32),
        ],
        compiler_params=params(),
        name="leaf",
    )(*parts, *bases, *targets)


def whole(target_ref, mine_ref, other_ref):
    half = BLOCK // 2
    core = lax.axis_index("row") & 1
    target_ref[pl.ds(pl.multiple_of(core * half, half), half), :] = mine_ref[...]
    target_ref[pl.ds(pl.multiple_of((1 - core) * half, half), half), :] = other_ref[...]


def coefficients(own_ref, sib_ref, held):
    own_gram, sib_gram = own_ref[:, :BLOCK], sib_ref[:, :BLOCK]
    own_proj, sib_proj = own_ref[:, BLOCK:], sib_ref[:, BLOCK:]
    residual = own_proj - full_dot(own_gram, sib_proj)
    power = full_dot(own_gram, sib_gram)
    total = eye() + power
    power = full_dot(power, power)
    total = total + full_dot(power, total)
    power = full_dot(power, power)

    def norm(value):
        return jnp.max(jnp.sum(jnp.abs(value), axis=0, keepdims=True))

    held[0], held[1] = power, total + full_dot(power, total)

    def more(carry):
        return jnp.logical_and(carry[0] * carry[0] > ROUNDING, carry[1] < 40)

    def once(carry):
        power = full_dot(held[0], held[0])
        held[0] = power
        held[1] += full_dot(power, held[1])
        return norm(power), carry[1] + 1

    lax.while_loop(more, once, (norm(power), 0))
    sib_z = full_dot(held[1], residual)
    return sib_proj - full_dot(sib_gram, sib_z), sib_z


def level_kernel(own_ref, mine_ref, other_ref, sib_ref, own_z_ref, sib_z_ref, held_ref):
    whole(sib_ref, mine_ref, other_ref)
    own_z_ref[...], sib_z_ref[...] = coefficients(own_ref, sib_ref, held_ref)


def level_step(own, mine, other):
    width = own.shape[1]
    return pl.pallas_call(
        level_kernel,
        out_shape=[
            shape_of(BLOCK, width),
            shape_of(BLOCK, width - BLOCK),
            shape_of(BLOCK, width - BLOCK),
        ],
        scratch_shapes=[pltpu.VMEM((2, BLOCK, BLOCK), F32)],
        compiler_params=params(),
        name="level",
    )(own, mine, other)


def parent_kernel(
    own_ref, sib_ref, own_z_ref, sib_z_ref, rest_ref, mine_ref, other_ref, *refs, level, levels
):
    first_ref, first_half_ref = refs[:2]
    last = level + 2 == levels
    sib_rest_ref = refs[-1]
    whole(sib_rest_ref, mine_ref, other_ref)
    half = BLOCK // 2
    core = lax.axis_index("row") & 1
    half_rows = pl.ds(pl.multiple_of(core * half, half), half)
    both_z = jnp.concatenate([own_z_ref[...], sib_z_ref[...]], axis=0)
    start = 0
    for row in range(level + 1, levels):
        span = (levels + 1 - row) * BLOCK
        here = slice(start, start + span)
        at = cols(row - level)
        left = jnp.concatenate([own_ref[:, at].T, sib_ref[:, at].T], axis=1)
        value = (rest_ref[:, here] + sib_rest_ref[:, here]) - full_dot(
            left, both_z[:, (row - level - 1) * BLOCK :]
        )
        if row == level + 1:
            first_ref[...] = value
        else:
            refs[2][:, start - first_ref.shape[1] : start - first_ref.shape[1] + span] = value
        start += span
    first_half_ref[...] = first_ref[half_rows, :]
    if not last:
        refs[3][...] = refs[2][half_rows, :]


def parent_step(own, sib, own_z, sib_z, rest, mine, other, level, levels):
    width = (levels - level) * BLOCK
    out_shape = [shape_of(BLOCK, width), shape_of(BLOCK // 2, width)]
    after = rest_width(level + 1, levels)
    if after:
        out_shape += [shape_of(BLOCK, after), shape_of(BLOCK // 2, after)]
    return pl.pallas_call(
        functools.partial(parent_kernel, level=level, levels=levels),
        out_shape=out_shape,
        scratch_shapes=[pltpu.VMEM(rest.shape, F32)],
        compiler_params=params(),
        name="parent",
    )(own, sib, own_z, sib_z, rest, mine, other)


def update_kernel(x_ref, z_ref, out_ref):
    out_ref[...] = x_ref[:, BLOCK:] - full_dot(x_ref[:, :BLOCK], z_ref[...])


def update(current, own_z):
    return pl.pallas_call(
        update_kernel,
        out_shape=shape_of(current.shape[0], current.shape[1] - BLOCK),
        compiler_params=params(),
        name="update",
    )(current, own_z)


def final_kernel(own_ref, mine_ref, other_ref, x_ref, out_ref, sib_ref, held_ref):
    whole(sib_ref, mine_ref, other_ref)
    own_z, _ = coefficients(own_ref, sib_ref, held_ref)
    out_ref[...] = x_ref[:, BLOCK:] - full_dot(x_ref[:, :BLOCK], own_z)


def final_step(own, mine, other, current):
    return pl.pallas_call(
        final_kernel,
        out_shape=shape_of(current.shape[0], BLOCK),
        scratch_shapes=[pltpu.VMEM(own.shape, F32), pltpu.VMEM((2, BLOCK, BLOCK), F32)],
        compiler_params=params(),
        name="final",
    )(own, mine, other, current)


def on_device(coords, order, targets, bases):
    levels = bases.shape[0]
    rows = targets.shape[0]
    leaf_size = rows * lax.axis_size("row")
    scales = tuple(float((leaf_size * 2**level) ** (-0.5)) for level in range(levels))
    orders = [order] + [swap(order, mask) for mask in (1, 2, 3)]
    chip_bases, chip_targets = swap(bases, 2), swap(targets, 2)
    own = jnp.pad(coords.reshape(6, BLOCK), ((0, 2), (0, 0)))
    leaves = lax.axis_size("leaf")
    table = lax.all_to_all(
        jnp.broadcast_to(own[None], (leaves, 8, BLOCK)), "leaf", 0, 0, tiled=True
    )
    order_row = jnp.concatenate(orders[::-1]).reshape(1, leaf_size)
    part = lookup(order_row, table)
    parts = [part] + [swap(part, mask) for mask in (1, 2, 3)]
    all_bases = [swap(chip_bases, 1), chip_bases, swap(bases, 1), bases]
    all_targets = [swap(chip_targets, 1), chip_targets, swap(targets, 1), targets]
    first, first_half, rest, rest_half, current = leaf(parts, all_bases, all_targets, scales)
    for level in range(levels):
        mine = swap(first_half, 4 << level)
        other = swap(mine, 1)
        if level + 1 == levels:
            return final_step(first, mine, other, current)
        mine, rest_half = lax.optimization_barrier((mine, rest_half))
        rest_mine = swap(rest_half, 4 << level)
        rest_other = swap(rest_mine, 1)
        sib, own_z, sib_z = level_step(first, mine, other)
        new = parent_step(first, sib, own_z, sib_z, rest, rest_mine, rest_other, level, levels)
        current = update(current, own_z)
        first, first_half = new[:2]
        if len(new) > 2:
            rest, rest_half = new[2:]


def solution(mesh):
    return jax.shard_map(
        on_device,
        mesh=mesh,
        in_specs=(
            P(None, AXES),
            P(AXES),
            P(AXES, None),
            P(None, AXES, None),
        ),
        out_specs=P(AXES, None),
        check_vma=False,
    )
```

```python
import functools

import jax
import jax.numpy as jnp
from jax import lax
from jax.experimental import pallas as pl
from jax.experimental.pallas import tpu as pltpu
from jax.sharding import PartitionSpec as P

LENGTH_SCALE = 0.1
NOISE_VAR = 1.0
BLOCK = 128
HALF = 64
ROUNDING = 3e-8
AXES = ("leaf", "row")
F32 = jnp.float32


def params():
    return pltpu.CompilerParams(vmem_limit_bytes=48 * 1024 * 1024)


def cost(microseconds):
    return pl.CostEstimate(
        flops=int(microseconds * 1.15e9),
        bytes_accessed=int(microseconds * 3.6e6),
        transcendentals=0,
    )


def swap(value, mask):
    count = lax.axis_size(AXES)
    return lax.ppermute(value, AXES, [(index, index ^ mask) for index in range(count)])


def split(value):
    high = value.astype(jnp.bfloat16)
    return high, (value - high.astype(F32)).astype(jnp.bfloat16)


def full_dot(left, right):
    return jnp.dot(left, right, preferred_element_type=F32, precision=lax.Precision.HIGHEST)


def half_dot(left, right):
    return jnp.dot(left, right, preferred_element_type=F32)


def eye():
    rows = lax.broadcasted_iota(jnp.int32, (BLOCK, BLOCK), 0)
    cols = lax.broadcasted_iota(jnp.int32, (BLOCK, BLOCK), 1)
    return (rows == cols).astype(F32)


def cols(index, count=1):
    return slice(index * BLOCK, (index + count) * BLOCK)


def spread_kernel(coords_ref, beside_ref, out_ref):
    copies = out_ref.shape[0]
    for at, ref in enumerate((coords_ref, beside_ref)):
        for row in range(6):
            piece = ref[row // 2 : row // 2 + 1, cols(row % 2)]
            out_ref[:, 8 * at + row, :] = jnp.broadcast_to(piece, (copies, BLOCK))
        out_ref[:, 8 * at + 6 : 8 * at + 8, :] = jnp.zeros((copies, 2, BLOCK), F32)


def spread(coords, beside, copies):
    return pl.pallas_call(
        spread_kernel,
        out_shape=shape_of(copies, 16, BLOCK),
        compiler_params=params(),
        cost_estimate=cost(1),
        name="spread",
    )(coords, beside)


def lookup_kernel(order_ref, table_ref, out_ref):
    mine = lax.axis_index("row")
    side = lax.axis_index("leaf") & 1
    numbers = order_ref[...]
    owner = numbers >> 8
    leaf_of = owner >> 2
    count = table_ref.shape[0]
    far = (leaf_of & 1) ^ side
    key = (2 * far + ((numbers >> 7) & 1)) * count + (leaf_of >> 1)
    key = jnp.where((owner & 3) == mine, key, -1)
    shape = (4 * count, numbers.shape[1])
    chosen = (lax.broadcasted_iota(jnp.int32, shape, 0) == key).astype(F32)
    lane = lax.broadcasted_iota(jnp.int32, (BLOCK, numbers.shape[1]), 0) == (numbers & 127)
    out_ref[...] = jnp.zeros_like(out_ref)
    for part in range(3):
        rows = (2 * part, 2 * part + 1, 8 + 2 * part, 9 + 2 * part)
        piece = jnp.concatenate([table_ref[:, row, :] for row in rows], axis=0)
        found = full_dot(piece.T, chosen)
        out_ref[part : part + 1, :] = jnp.sum(jnp.where(lane, found, 0.0), axis=0, keepdims=True)


def lookup(order_row, table):
    return pl.pallas_call(
        lookup_kernel,
        out_shape=jax.ShapeDtypeStruct((8, order_row.shape[1]), F32),
        compiler_params=params(),
        cost_estimate=cost(1.5),
        name="lookup",
    )(order_row, table)


def pivot_inverse(pivot, largest, held):
    scale = 2.0 / (largest + 1.0)
    cheb = (largest + 1.0) / (largest - 1.0)
    residual = eye() - scale * pivot
    total = None
    for step in range(5):
        if step:
            total = total + full_dot(residual_now, total)
        else:
            total = eye() + residual
        doubled = 2.0 * cheb * cheb - 1.0
        grow, drop = (doubled + 1.0) / doubled, 1.0 / doubled
        scale = scale * grow
        cheb = doubled
        if step < 4:
            residual = grow * full_dot(residual, residual) - drop * eye()
            residual_now = residual
    held[0], held[1] = residual, scale * total

    def once(carry):
        before, now = carry
        doubled = 2.0 * before * before - 1.0
        residual = (doubled + 1.0) / doubled * full_dot(held[0], held[0]) - eye() / doubled
        held[0] = residual
        doubled = 2.0 * now * now - 1.0
        held[1] = (doubled + 1.0) / doubled * (held[1] + full_dot(residual, held[1]))
        return now, doubled

    bound = jnp.max(cheb)
    lax.while_loop(
        lambda carry: carry[1] * ROUNDING < 1.0, once, (jnp.sqrt((bound + 1.0) * 0.5), bound)
    )
    return held[1]


def leaf_kernel(
    own_ref, core_ref, chip_ref, far_ref, *refs, levels, scales
):
    basis_refs, target_refs = refs[:4], refs[4:8]
    first_ref, next_ref, later_ref, own_x_ref = refs[8:12]
    mat_ref, rhs_ref, sol_ref, held_ref = refs[12:16]
    size = mat_ref.shape[0]
    blocks = size // BLOCK
    piece = size // 4
    width = rhs_ref.shape[1]
    core = lax.axis_index("row") & 1
    pieces = []
    for spot in range(4):
        total = own_ref[:, spot * piece : (spot + 1) * piece]
        for mask, ref in ((1, core_ref), (2, chip_ref), (3, far_ref)):
            other = spot ^ mask
            total = total + ref[:, other * piece : (other + 1) * piece]
        pieces.append(total)
    points = jnp.concatenate(pieces, axis=1)
    for spot in range(4):
        rows = slice(spot * piece, (spot + 1) * piece)
        for level in range(levels):
            rhs_ref[rows, cols(level)] = basis_refs[spot][level] * scales[level]
        rhs_ref[rows, cols(levels)] = target_refs[spot][...]
    largest = []
    for block in range(blocks):
        turned = points[:, cols(block)].T
        squared = jnp.zeros((BLOCK, size), F32)
        for part in range(3):
            offset = turned[:, part : part + 1] - points[part : part + 1, :]
            squared = squared + offset * offset
        value = jnp.exp(squared * (-0.5 / (LENGTH_SCALE * LENGTH_SCALE)))
        mat_ref[cols(block), :] = value
        value = value[:, cols(block)] + NOISE_VAR * eye()
        mat_ref[cols(block), cols(block)] = value
        sums = jnp.sum(value, axis=0, keepdims=True)
        largest.append(jnp.max(sums, axis=1, keepdims=True) + 0.01)
    pivot = mat_ref[cols(0), cols(0)]
    right = None
    for block in range(blocks):
        inverse = pivot_inverse(pivot, largest[block], held_ref)
        after = blocks - block - 1
        solved = full_dot(inverse, rhs_ref[cols(block), :])
        sol_ref[cols(block), :] = solved
        if after == 0:
            break
        right = full_dot(inverse, mat_ref[cols(block), cols(block + 1, after)])
        down = mat_ref[cols(block + 1, after), cols(block)]
        pivot = mat_ref[cols(block + 1), cols(block + 1)] - full_dot(
            down[:BLOCK], right[:, :BLOCK]
        )
        high, low = split(down)
        left = jnp.concatenate([high, high, low], axis=1)
        high, low = split(right)
        mat_ref[cols(block + 1, after), cols(block + 1, after)] -= half_dot(
            left, jnp.concatenate([high, low, high], axis=0)
        )
        high, low = split(solved)
        rhs_ref[cols(block + 1, after), :] -= half_dot(
            left, jnp.concatenate([high, low, high], axis=0)
        )
    own_x_ref[cols(1), :] = sol_ref[cols(blocks - 1), :]
    own_x_ref[cols(0), :] = sol_ref[cols(blocks - 2), :] - full_dot(
        right, sol_ref[cols(blocks - 1), :]
    )
    high, low = split(sol_ref[...])
    lefts = []
    for level in range(levels):
        turned = rhs_ref[:, cols(level)].T
        lefts.append(jnp.where(core == 0, turned[:HALF], turned[HALF:]))
    left_high, left_low = split(jnp.concatenate(lefts, axis=0))
    rows = levels * HALF
    both = half_dot(jnp.concatenate([left_high, left_low], axis=0), high)
    sums = both[:rows] + (both[rows:] + half_dot(left_high, low))
    start = 0
    for level in range(levels):
        value = sums[level * HALF : (level + 1) * HALF, level * BLOCK :]
        if level == 0:
            first_ref[...] = value
        elif level == 1:
            next_ref[...] = value
        else:
            later_ref[:, start : start + value.shape[1]] = value
            start += value.shape[1]


def later_width(level, levels):
    return sum((levels + 1 - row) * BLOCK for row in range(level + 2, levels))


def shape_of(*shape):
    return jax.ShapeDtypeStruct(shape, F32)


def leaf(parts, bases, targets, scales):
    levels = len(scales)
    size = parts[0].shape[1]
    width = (levels + 1) * BLOCK
    return pl.pallas_call(
        functools.partial(leaf_kernel, levels=levels, scales=scales),
        out_shape=[
            shape_of(HALF, width),
            shape_of(HALF, width - BLOCK),
            shape_of(HALF, later_width(0, levels)),
            shape_of(2 * BLOCK, width),
        ],
        scratch_shapes=[
            pltpu.VMEM((size, size), F32),
            pltpu.VMEM((size, width), F32),
            pltpu.VMEM((size, width), F32),
            pltpu.VMEM((2, BLOCK, BLOCK), F32),
        ],
        compiler_params=params(),
        cost_estimate=cost(30),
        name="leaf",
    )(*parts, *bases, *targets)


def whole(target_ref, mine_ref, other_ref):
    core = lax.axis_index("row") & 1
    target_ref[pl.ds(pl.multiple_of(core * HALF, HALF), HALF), :] = mine_ref[...]
    target_ref[pl.ds(pl.multiple_of((1 - core) * HALF, HALF), HALF), :] = other_ref[...]


def coefficients(own_ref, sib_ref, held):
    own_gram, sib_gram = own_ref[:, :BLOCK], sib_ref[:, :BLOCK]
    own_proj, sib_proj = own_ref[:, BLOCK:], sib_ref[:, BLOCK:]
    power = full_dot(own_gram, sib_gram)
    residual = own_proj - full_dot(own_gram, sib_proj)
    total = eye() + power
    power = full_dot(power, power)
    total = total + full_dot(power, total)
    power = full_dot(power, power)

    def norm(value):
        return jnp.max(jnp.sum(jnp.abs(value), axis=0, keepdims=True))

    held[0], held[1] = power, total + full_dot(power, total)

    def more(carry):
        return jnp.logical_and(carry[0] * carry[0] > ROUNDING, carry[1] < 40)

    def once(carry):
        power = full_dot(held[0], held[0])
        held[0] = power
        held[1] += full_dot(power, held[1])
        return norm(power), carry[1] + 1

    lax.while_loop(more, once, (norm(power), 0))
    sib_z = full_dot(held[1], residual)
    return sib_proj - full_dot(sib_gram, sib_z), sib_z


def level_kernel(*refs):
    own_mine_ref, own_other_ref, mine_ref, other_ref = refs[:4]
    own_ref, sib_ref, own_z_ref, sib_z_ref, held_ref = refs[4:]
    whole(own_ref, own_mine_ref, own_other_ref)
    whole(sib_ref, mine_ref, other_ref)
    own_z_ref[...], sib_z_ref[...] = coefficients(own_ref, sib_ref, held_ref)


def level_step(own_mine, own_other, mine, other):
    width = mine.shape[1]
    return pl.pallas_call(
        level_kernel,
        out_shape=[shape_of(BLOCK, width)] * 2 + [shape_of(BLOCK, width - BLOCK)] * 2,
        scratch_shapes=[pltpu.VMEM((2, BLOCK, BLOCK), F32)],
        compiler_params=params(),
        cost_estimate=cost(2),
        name="level",
    )(own_mine, own_other, mine, other)


def half_turned(own_ref, sib_ref, at):
    core = lax.axis_index("row") & 1
    turned = jnp.concatenate([own_ref[:, at].T, sib_ref[:, at].T], axis=1)
    return jnp.where(core == 0, turned[:HALF], turned[HALF:])


def next_kernel(own_ref, sib_ref, own_z_ref, sib_z_ref, row_ref, sib_row_ref, out_ref):
    both_z = jnp.concatenate([own_z_ref[...], sib_z_ref[...]], axis=0)
    left = half_turned(own_ref, sib_ref, cols(1))
    out_ref[...] = (row_ref[...] + sib_row_ref[...]) - full_dot(left, both_z)


def next_step(whole_rows, row, sib_row):
    return pl.pallas_call(
        next_kernel,
        out_shape=shape_of(*row.shape),
        compiler_params=params(),
        cost_estimate=cost(1),
        name="next",
    )(*whole_rows, row, sib_row)


def later_kernel(*refs, level, levels):
    own_ref, sib_ref, own_z_ref, sib_z_ref, x_ref, rest_ref, sib_rest_ref = refs[:7]
    x_out_ref, next_ref = refs[7:9]
    x_out_ref[...] = x_ref[:, BLOCK:] - full_dot(x_ref[:, :BLOCK], own_z_ref[...])
    both_z = jnp.concatenate([own_z_ref[...], sib_z_ref[...]], axis=0)
    start = 0
    for row in range(level + 2, levels):
        span = (levels + 1 - row) * BLOCK
        here = slice(start, start + span)
        left = half_turned(own_ref, sib_ref, cols(row - level))
        value = (rest_ref[:, here] + sib_rest_ref[:, here]) - full_dot(
            left, both_z[:, (row - level - 1) * BLOCK :]
        )
        if row == level + 2:
            next_ref[...] = value
            skipped = span
        else:
            refs[9][:, start - skipped : start - skipped + span] = value
        start += span


def later_step(whole_rows, current, rest, sib_rest, level, levels):
    out_shape = [
        shape_of(current.shape[0], current.shape[1] - BLOCK),
        shape_of(HALF, (levels - level - 1) * BLOCK),
    ]
    after = later_width(level + 1, levels)
    if after:
        out_shape.append(shape_of(HALF, after))
    return pl.pallas_call(
        functools.partial(later_kernel, level=level, levels=levels),
        out_shape=out_shape,
        compiler_params=params(),
        cost_estimate=cost(2),
        name="later",
    )(*whole_rows, current, rest, sib_rest)


def final_kernel(*refs):
    own_mine_ref, own_other_ref, mine_ref, other_ref, x_ref, before_z_ref, out_ref = refs[:7]
    own_ref, sib_ref, held_ref = refs[7:]
    whole(own_ref, own_mine_ref, own_other_ref)
    whole(sib_ref, mine_ref, other_ref)
    current = x_ref[:, BLOCK:] - full_dot(x_ref[:, :BLOCK], before_z_ref[...])
    own_z, _ = coefficients(own_ref, sib_ref, held_ref)
    out_ref[...] = current[:, BLOCK:] - full_dot(current[:, :BLOCK], own_z)


def final_step(own_mine, own_other, mine, other, current, before_z):
    whole_row = pltpu.VMEM((BLOCK, mine.shape[1]), F32)
    return pl.pallas_call(
        final_kernel,
        out_shape=shape_of(current.shape[0], BLOCK),
        scratch_shapes=[whole_row, whole_row, pltpu.VMEM((2, BLOCK, BLOCK), F32)],
        compiler_params=params(),
        cost_estimate=cost(2),
        name="final",
    )(own_mine, own_other, mine, other, current, before_z)


PARTNERS = (4 | 2, 8, 16 | 8, 32, 64, 128 | 64 | 32)


def on_device(coords, order, targets, bases):
    levels = bases.shape[0]
    rows = targets.shape[0]
    leaf_size = rows * lax.axis_size("row")
    scales = tuple(float((leaf_size * 2**level) ** (-0.5)) for level in range(levels))
    orders = [order] + [swap(order, mask) for mask in (1, 2, 3)]
    chip_bases, chip_targets = swap(bases, 2), swap(targets, 2)
    beside = swap(coords, 4)
    half = lax.axis_size("leaf") // 2
    groups = [[2 * index + side for index in range(half)] for side in range(2)]
    beside, *orders = lax.optimization_barrier((beside, *orders))
    table = lax.all_to_all(
        spread(coords, beside, half), "leaf", 0, 0, axis_index_groups=groups, tiled=True
    )
    order_row = jnp.concatenate(orders[::-1]).reshape(1, leaf_size)
    part = lookup(order_row, table)
    chip_bases, chip_targets, _ = lax.optimization_barrier((chip_bases, chip_targets, part))
    parts = [part] + [swap(part, mask) for mask in (1, 2, 3)]
    all_bases = [swap(chip_bases, 1), chip_bases, swap(bases, 1), bases]
    all_targets = [swap(chip_targets, 1), chip_targets, swap(targets, 1), targets]
    own, coming, later, current = leaf(parts, all_bases, all_targets, scales)
    for level in range(levels):
        mask = PARTNERS[level]
        mine = swap(own, mask)
        own_other = swap(own, 1)
        other = swap(mine, 1)
        if level + 1 == levels:
            return final_step(own, own_other, mine, other, current, own_z)
        coming, _ = lax.optimization_barrier((coming, mine))
        sib_coming = swap(coming, mask)
        whole_rows = level_step(own, own_other, mine, other)
        own_z = whole_rows[2]
        if later is not None:
            sib_coming, own_z, later = lax.optimization_barrier((sib_coming, own_z, later))
            sib_later = swap(later, mask)
        own = next_step(whole_rows, coming, sib_coming)
        if later is not None:
            sib_later, _ = lax.optimization_barrier((sib_later, own))
            new = later_step(whole_rows, current, later, sib_later, level, levels)
            current, coming = new[:2]
            later = new[2] if len(new) > 2 else None


def solution(mesh):
    return jax.shard_map(
        on_device,
        mesh=mesh,
        in_specs=(
            P(None, AXES),
            P(AXES),
            P(AXES, None),
            P(None, AXES, None),
        ),
        out_specs=P(AXES, None),
        check_vma=False,
    )
```

```python
import functools

import jax
import jax.numpy as jnp
from jax import lax
from jax.experimental import pallas as pl
from jax.experimental.pallas import tpu as pltpu
from jax.sharding import PartitionSpec as P

LENGTH_SCALE = 0.1
NOISE_VAR = 1.0
BLOCK = 128
HALF = 64
ROUNDING = 3e-8
AXES = ("leaf", "row")
F32 = jnp.float32


def params():
    return pltpu.CompilerParams(vmem_limit_bytes=48 * 1024 * 1024)


def cost(microseconds):
    return pl.CostEstimate(
        flops=int(microseconds * 1.15e9),
        bytes_accessed=int(microseconds * 3.6e6),
        transcendentals=0,
    )


def swap(value, mask):
    count = lax.axis_size(AXES)
    return lax.ppermute(value, AXES, [(index, index ^ mask) for index in range(count)])


def split(value):
    high = value.astype(jnp.bfloat16)
    return high, (value - high.astype(F32)).astype(jnp.bfloat16)


def full_dot(left, right):
    return jnp.dot(left, right, preferred_element_type=F32, precision=lax.Precision.HIGHEST)


def half_dot(left, right):
    return jnp.dot(left, right, preferred_element_type=F32)


def three_dot(left, right):
    high, low = split(left)
    right_high, right_low = split(right)
    return half_dot(
        jnp.concatenate([high, high, low], axis=1),
        jnp.concatenate([right_high, right_low, right_high], axis=0),
    )


def eye():
    rows = lax.broadcasted_iota(jnp.int32, (BLOCK, BLOCK), 0)
    cols = lax.broadcasted_iota(jnp.int32, (BLOCK, BLOCK), 1)
    return (rows == cols).astype(F32)


def cols(index, count=1):
    return slice(index * BLOCK, (index + count) * BLOCK)


def spread_kernel(coords_ref, beside_ref, out_ref):
    copies = out_ref.shape[0]
    for at, ref in enumerate((coords_ref, beside_ref)):
        for row in range(6):
            piece = ref[row // 2 : row // 2 + 1, cols(row % 2)]
            out_ref[:, 8 * at + row, :] = jnp.broadcast_to(piece, (copies, BLOCK))
        out_ref[:, 8 * at + 6 : 8 * at + 8, :] = jnp.zeros((copies, 2, BLOCK), F32)


def spread(coords, beside, copies):
    return pl.pallas_call(
        spread_kernel,
        out_shape=shape_of(copies, 16, BLOCK),
        compiler_params=params(),
        cost_estimate=cost(1),
        name="spread",
    )(coords, beside)


def lookup_kernel(order_ref, table_ref, out_ref):
    mine = lax.axis_index("row")
    side = lax.axis_index("leaf") & 1
    numbers = order_ref[...]
    owner = numbers >> 8
    leaf_of = owner >> 2
    count = table_ref.shape[0]
    far = (leaf_of & 1) ^ side
    key = (2 * far + ((numbers >> 7) & 1)) * count + (leaf_of >> 1)
    key = jnp.where((owner & 3) == mine, key, -1)
    shape = (4 * count, numbers.shape[1])
    chosen = (lax.broadcasted_iota(jnp.int32, shape, 0) == key).astype(F32)
    lane = lax.broadcasted_iota(jnp.int32, (BLOCK, numbers.shape[1]), 0) == (numbers & 127)
    out_ref[...] = jnp.zeros_like(out_ref)
    for part in range(3):
        rows = (2 * part, 2 * part + 1, 8 + 2 * part, 9 + 2 * part)
        piece = jnp.concatenate([table_ref[:, row, :] for row in rows], axis=0)
        found = full_dot(piece.T, chosen)
        out_ref[part : part + 1, :] = jnp.sum(jnp.where(lane, found, 0.0), axis=0, keepdims=True)


def lookup(order_row, table):
    return pl.pallas_call(
        lookup_kernel,
        out_shape=jax.ShapeDtypeStruct((8, order_row.shape[1]), F32),
        compiler_params=params(),
        cost_estimate=cost(1.5),
        name="lookup",
    )(order_row, table)


def pivot_inverse(pivot, largest, held, between):
    scale = 2.0 / (largest + 1.0)
    cheb = (largest + 1.0) / (largest - 1.0)
    residual = eye() - scale * pivot
    total = None
    for step in range(5):
        if step:
            total = total + full_dot(residual_now, total)
        else:
            total = eye() + residual
        doubled = 2.0 * cheb * cheb - 1.0
        grow, drop = (doubled + 1.0) / doubled, 1.0 / doubled
        scale = scale * grow
        cheb = doubled
        if step < 4:
            residual = grow * full_dot(residual, residual) - drop * eye()
            residual_now = residual
        for piece in between[step::5]:
            piece()
    held[0], held[1] = residual, scale * total

    def once(carry):
        before, now = carry
        doubled = 2.0 * before * before - 1.0
        residual = (doubled + 1.0) / doubled * full_dot(held[0], held[0]) - eye() / doubled
        held[0] = residual
        doubled = 2.0 * now * now - 1.0
        held[1] = (doubled + 1.0) / doubled * (held[1] + full_dot(residual, held[1]))
        return now, doubled

    bound = jnp.max(cheb)
    lax.while_loop(
        lambda carry: carry[1] * ROUNDING < 1.0, once, (jnp.sqrt((bound + 1.0) * 0.5), bound)
    )
    return held[1]


def leaf_kernel(
    own_ref, core_ref, chip_ref, far_ref, *refs, levels, scales
):
    basis_refs, target_refs = refs[:4], refs[4:8]
    first_ref, next_ref, soon_ref, rest_ref, own_x_ref = refs[8:13]
    mat_ref, rhs_ref, sol_ref, held_ref = refs[13:17]
    size = mat_ref.shape[0]
    blocks = size // BLOCK
    piece = size // 4
    width = rhs_ref.shape[1]
    core = lax.axis_index("row") & 1
    pieces = []
    for spot in range(4):
        total = own_ref[:, spot * piece : (spot + 1) * piece]
        for mask, ref in ((1, core_ref), (2, chip_ref), (3, far_ref)):
            other = spot ^ mask
            total = total + ref[:, other * piece : (other + 1) * piece]
        pieces.append(total)
    points = jnp.concatenate(pieces, axis=1)
    for spot in range(4):
        rows = slice(spot * piece, (spot + 1) * piece)
        for level in range(levels):
            rhs_ref[rows, cols(level)] = basis_refs[spot][level] * scales[level]
        rhs_ref[rows, cols(levels)] = target_refs[spot][...]
    largest = []
    for block in range(blocks):
        turned = points[:, cols(block)].T
        squared = jnp.zeros((BLOCK, size), F32)
        for part in range(3):
            offset = turned[:, part : part + 1] - points[part : part + 1, :]
            squared = squared + offset * offset
        value = jnp.exp(squared * (-0.5 / (LENGTH_SCALE * LENGTH_SCALE)))
        mat_ref[cols(block), :] = value
        value = value[:, cols(block)] + NOISE_VAR * eye()
        mat_ref[cols(block), cols(block)] = value
        sums = jnp.sum(value, axis=0, keepdims=True)
        largest.append(jnp.max(sums, axis=1, keepdims=True) + 0.01)
    pivot = mat_ref[cols(0), cols(0)]
    right = None
    between = []
    for block in range(blocks):
        inverse = pivot_inverse(pivot, largest[block], held_ref, between)
        after = blocks - block - 1
        solved = three_dot(inverse, rhs_ref[cols(block), :])
        sol_ref[cols(block), :] = solved
        if after == 0:
            break
        right = three_dot(inverse, mat_ref[cols(block), cols(block + 1, after)])
        down = mat_ref[cols(block + 1, after), cols(block)]
        pivot = mat_ref[cols(block + 1), cols(block + 1)] - full_dot(
            down[:BLOCK], right[:, :BLOCK]
        )
        high, low = split(down)
        left = jnp.concatenate([high, high, low], axis=1)
        high, low = split(right)
        mat_right = jnp.concatenate([high, low, high], axis=0)
        high, low = split(solved)
        rhs_right = jnp.concatenate([high, low, high], axis=0)

        def piece(index, block=block, left=left, mat_right=mat_right, rhs_right=rhs_right):
            row = cols(block + 1 + index)
            part = left[cols(index)]
            mat_ref[row, cols(block + 1, blocks - block - 1)] -= half_dot(part, mat_right)
            rhs_ref[row, :] -= half_dot(part, rhs_right)

        between = [functools.partial(piece, index) for index in range(after)]
    own_x_ref[cols(1), :] = sol_ref[cols(blocks - 1), :]
    own_x_ref[cols(0), :] = sol_ref[cols(blocks - 2), :] - full_dot(
        right, sol_ref[cols(blocks - 1), :]
    )
    high, low = split(sol_ref[...])
    lefts = []
    for level in range(levels):
        turned = rhs_ref[:, cols(level)].T
        lefts.append(jnp.where(core == 0, turned[:HALF], turned[HALF:]))
    left_high, left_low = split(jnp.concatenate(lefts, axis=0))
    rows = levels * HALF
    both = half_dot(jnp.concatenate([left_high, left_low], axis=0), high)
    sums = both[:rows] + (both[rows:] + half_dot(left_high, low))
    start = 0
    for level in range(levels):
        value = sums[level * HALF : (level + 1) * HALF, level * BLOCK :]
        if level == 0:
            first_ref[...] = value
        elif level == 1:
            next_ref[...] = value
        elif level == 2:
            soon_ref[...] = value
        else:
            rest_ref[:, start : start + value.shape[1]] = value
            start += value.shape[1]


def rest_width(level, levels):
    return sum((levels + 1 - row) * BLOCK for row in range(level + 3, levels))


def shape_of(*shape):
    return jax.ShapeDtypeStruct(shape, F32)


def leaf(parts, bases, targets, scales):
    levels = len(scales)
    size = parts[0].shape[1]
    width = (levels + 1) * BLOCK
    return pl.pallas_call(
        functools.partial(leaf_kernel, levels=levels, scales=scales),
        out_shape=[
            shape_of(HALF, width),
            shape_of(HALF, width - BLOCK),
            shape_of(HALF, width - 2 * BLOCK),
            shape_of(HALF, rest_width(0, levels)),
            shape_of(2 * BLOCK, width),
        ],
        scratch_shapes=[
            pltpu.VMEM((size, size), F32),
            pltpu.VMEM((size, width), F32),
            pltpu.VMEM((size, width), F32),
            pltpu.VMEM((2, BLOCK, BLOCK), F32),
        ],
        compiler_params=params(),
        cost_estimate=cost(30),
        name="leaf",
    )(*parts, *bases, *targets)


def whole(target_ref, mine_ref, other_ref):
    core = lax.axis_index("row") & 1
    target_ref[pl.ds(pl.multiple_of(core * HALF, HALF), HALF), :] = mine_ref[...]
    target_ref[pl.ds(pl.multiple_of((1 - core) * HALF, HALF), HALF), :] = other_ref[...]


def coefficients(own_ref, sib_ref, held):
    own_gram, sib_gram = own_ref[:, :BLOCK], sib_ref[:, :BLOCK]
    own_proj, sib_proj = own_ref[:, BLOCK:], sib_ref[:, BLOCK:]
    power = full_dot(own_gram, sib_gram)
    residual = own_proj - full_dot(own_gram, sib_proj)
    total = eye() + power
    power = full_dot(power, power)
    total = total + full_dot(power, total)
    power = full_dot(power, power)

    def norm(value):
        return jnp.max(jnp.sum(jnp.abs(value), axis=0, keepdims=True))

    held[0], held[1] = power, total + full_dot(power, total)

    def more(carry):
        return jnp.logical_and(carry[0] * carry[0] > ROUNDING, carry[1] < 40)

    def once(carry):
        power = full_dot(held[0], held[0])
        held[0] = power
        held[1] += full_dot(power, held[1])
        return norm(power), carry[1] + 1

    lax.while_loop(more, once, (norm(power), 0))
    sib_z = full_dot(held[1], residual)
    return sib_proj - full_dot(sib_gram, sib_z), sib_z


def level_kernel(*refs):
    own_mine_ref, own_other_ref, mine_ref, other_ref = refs[:4]
    own_ref, sib_ref, own_z_ref, sib_z_ref, held_ref = refs[4:]
    whole(own_ref, own_mine_ref, own_other_ref)
    whole(sib_ref, mine_ref, other_ref)
    own_z_ref[...], sib_z_ref[...] = coefficients(own_ref, sib_ref, held_ref)


def level_step(own_mine, own_other, mine, other):
    width = mine.shape[1]
    return pl.pallas_call(
        level_kernel,
        out_shape=[shape_of(BLOCK, width)] * 2 + [shape_of(BLOCK, width - BLOCK)] * 2,
        scratch_shapes=[pltpu.VMEM((2, BLOCK, BLOCK), F32)],
        compiler_params=params(),
        cost_estimate=cost(2),
        name="level",
    )(own_mine, own_other, mine, other)


def half_turned(own_ref, sib_ref, at):
    core = lax.axis_index("row") & 1
    turned = jnp.concatenate([own_ref[:, at].T, sib_ref[:, at].T], axis=1)
    return jnp.where(core == 0, turned[:HALF], turned[HALF:])


def parent_rows(refs, rest_ref, sib_rest_ref, rows, level, levels):
    own_ref, sib_ref, own_z_ref, sib_z_ref = refs
    both_z = jnp.concatenate([own_z_ref[...], sib_z_ref[...]], axis=0)
    start = 0
    for row in rows:
        span = (levels + 1 - row) * BLOCK
        here = slice(start, start + span)
        left = half_turned(own_ref, sib_ref, cols(row - level))
        yield (rest_ref[:, here] + sib_rest_ref[:, here]) - full_dot(
            left, both_z[:, (row - level - 1) * BLOCK :]
        )
        start += span


def row_kernel(*refs, row, level, levels, with_current):
    sums = parent_rows(refs[:4], refs[4], refs[5], [row], level, levels)
    if with_current:
        x_ref, out_ref, x_out_ref = refs[6:]
        x_out_ref[...] = x_ref[:, BLOCK:] - full_dot(x_ref[:, :BLOCK], refs[2][...])
    else:
        out_ref = refs[6]
    out_ref[...] = next(sums)


def row_step(whole_rows, mine, sib, row, level, levels, current=None):
    out_shape = [shape_of(*mine.shape)]
    operands = [*whole_rows, mine, sib]
    if current is not None:
        operands.append(current)
        out_shape.append(shape_of(current.shape[0], current.shape[1] - BLOCK))
    return pl.pallas_call(
        functools.partial(
            row_kernel, row=row, level=level, levels=levels, with_current=current is not None
        ),
        out_shape=out_shape,
        compiler_params=params(),
        cost_estimate=cost(1),
        name="row",
    )(*operands)


def rest_kernel(*refs, level, levels):
    x_ref, rest_ref, sib_rest_ref, x_out_ref, soon_ref = refs[4:9]
    rows = range(level + 3, levels)
    start = 0
    for row, value in zip(rows, parent_rows(refs[:4], rest_ref, sib_rest_ref, rows, level, levels)):
        if row == level + 3:
            soon_ref[...] = value
        else:
            refs[9][:, start : start + value.shape[1]] = value
            start += value.shape[1]
    x_out_ref[...] = x_ref[:, BLOCK:] - full_dot(x_ref[:, :BLOCK], refs[2][...])


def rest_step(whole_rows, current, rest, sib_rest, level, levels):
    out_shape = [
        shape_of(current.shape[0], current.shape[1] - BLOCK),
        shape_of(HALF, (levels - level - 2) * BLOCK),
    ]
    after = rest_width(level + 1, levels)
    if after:
        out_shape.append(shape_of(HALF, after))
    return pl.pallas_call(
        functools.partial(rest_kernel, level=level, levels=levels),
        out_shape=out_shape,
        compiler_params=params(),
        cost_estimate=cost(2),
        name="rest",
    )(*whole_rows, current, rest, sib_rest)


def final_kernel(*refs):
    own_mine_ref, own_other_ref, mine_ref, other_ref, x_ref, before_z_ref, out_ref = refs[:7]
    own_ref, sib_ref, held_ref = refs[7:]
    whole(own_ref, own_mine_ref, own_other_ref)
    whole(sib_ref, mine_ref, other_ref)
    current = x_ref[:, BLOCK:] - full_dot(x_ref[:, :BLOCK], before_z_ref[...])
    own_z, _ = coefficients(own_ref, sib_ref, held_ref)
    out_ref[...] = current[:, BLOCK:] - full_dot(current[:, :BLOCK], own_z)


def final_step(own_mine, own_other, mine, other, current, before_z):
    whole_row = pltpu.VMEM((BLOCK, mine.shape[1]), F32)
    return pl.pallas_call(
        final_kernel,
        out_shape=shape_of(current.shape[0], BLOCK),
        scratch_shapes=[whole_row, whole_row, pltpu.VMEM((2, BLOCK, BLOCK), F32)],
        compiler_params=params(),
        cost_estimate=cost(2),
        name="final",
    )(own_mine, own_other, mine, other, current, before_z)


PARTNERS = (4 | 2, 8, 16 | 8, 32, 64, 128 | 64 | 32)


def on_device(coords, order, targets, bases):
    levels = bases.shape[0]
    rows = targets.shape[0]
    leaf_size = rows * lax.axis_size("row")
    scales = tuple(float((leaf_size * 2**level) ** (-0.5)) for level in range(levels))
    orders = [order] + [swap(order, mask) for mask in (1, 2, 3)]
    beside = swap(coords, 4)
    half = lax.axis_size("leaf") // 2
    groups = [[2 * index + side for index in range(half)] for side in range(2)]
    beside, sent_bases, sent_targets, *orders = lax.optimization_barrier(
        (beside, bases, targets, *orders)
    )
    chip_bases, chip_targets = swap(sent_bases, 2), swap(sent_targets, 2)
    table = lax.all_to_all(
        spread(coords, beside, half), "leaf", 0, 0, axis_index_groups=groups, tiled=True
    )
    order_row = jnp.concatenate(orders[::-1]).reshape(1, leaf_size)
    part = lookup(order_row, table)
    chip_bases, chip_targets, _ = lax.optimization_barrier((chip_bases, chip_targets, part))
    parts = [part] + [swap(part, mask) for mask in (1, 2, 3)]
    all_bases = [swap(chip_bases, 1), chip_bases, swap(bases, 1), bases]
    all_targets = [swap(chip_targets, 1), chip_targets, swap(targets, 1), targets]
    own, coming, soon, rest, current = leaf(parts, all_bases, all_targets, scales)
    for level in range(levels):
        mask = PARTNERS[level]
        mine = swap(own, mask)
        own_other = swap(own, 1)
        other = swap(mine, 1)
        if level + 1 == levels:
            return final_step(own, own_other, mine, other, current, own_z)
        coming, _ = lax.optimization_barrier((coming, mine))
        sib_coming = swap(coming, mask)
        whole_rows = level_step(own, own_other, mine, other)
        own_z = whole_rows[2]
        own = row_step(whole_rows, coming, sib_coming, level + 1, level, levels)[0]
        if level + 2 == levels:
            continue
        soon, _ = lax.optimization_barrier((soon, own))
        sib_soon = swap(soon, mask)
        if level + 3 == levels:
            coming, current = row_step(
                whole_rows, soon, sib_soon, level + 2, level, levels, current
            )
            continue
        rest, _ = lax.optimization_barrier((rest, sib_soon))
        sib_rest = swap(rest, mask)
        coming = row_step(whole_rows, soon, sib_soon, level + 2, level, levels)[0]
        sib_rest, _ = lax.optimization_barrier((sib_rest, coming))
        new = rest_step(whole_rows, current, rest, sib_rest, level, levels)
        current, soon = new[:2]
        rest = new[2] if len(new) > 2 else None


def solution(mesh):
    return jax.shard_map(
        on_device,
        mesh=mesh,
        in_specs=(
            P(None, AXES),
            P(AXES),
            P(AXES, None),
            P(None, AXES, None),
        ),
        out_specs=P(AXES, None),
        check_vma=False,
    )
```

```python
import functools

import jax
import jax.numpy as jnp
from jax import lax
from jax.experimental import pallas as pl
from jax.experimental.pallas import tpu as pltpu
from jax.sharding import PartitionSpec as P

LENGTH_SCALE = 0.1
NOISE_VAR = 1.0
BLOCK = 128
HALF = 64
ROUNDING = 3e-8
FEW, FEW_LIMIT, MANY = 5, 12.0, 7
AXES = ("leaf", "row")
F32 = jnp.float32


def params():
    return pltpu.CompilerParams(vmem_limit_bytes=48 * 1024 * 1024)


def cost(microseconds):
    return pl.CostEstimate(
        flops=int(microseconds * 1.15e9),
        bytes_accessed=int(microseconds * 3.6e6),
        transcendentals=0,
    )


def swap(value, mask):
    count = lax.axis_size(AXES)
    return lax.ppermute(value, AXES, [(index, index ^ mask) for index in range(count)])


def split(value):
    high = value.astype(jnp.bfloat16)
    return high, (value - high.astype(F32)).astype(jnp.bfloat16)


def full_dot(left, right):
    return jnp.dot(left, right, preferred_element_type=F32, precision=lax.Precision.HIGHEST)


def half_dot(left, right):
    return jnp.dot(left, right, preferred_element_type=F32)


def three_dot(left, right):
    high, low = split(left)
    right_high, right_low = split(right)
    return half_dot(
        jnp.concatenate([high, high, low], axis=1),
        jnp.concatenate([right_high, right_low, right_high], axis=0),
    )


def eye():
    rows = lax.broadcasted_iota(jnp.int32, (BLOCK, BLOCK), 0)
    cols = lax.broadcasted_iota(jnp.int32, (BLOCK, BLOCK), 1)
    return (rows == cols).astype(F32)


def cols(index, count=1):
    return slice(index * BLOCK, (index + count) * BLOCK)


def spread_kernel(coords_ref, beside_ref, out_ref):
    copies = out_ref.shape[0]
    for at, ref in enumerate((coords_ref, beside_ref)):
        for row in range(6):
            piece = ref[row // 2 : row // 2 + 1, cols(row % 2)]
            out_ref[:, 8 * at + row, :] = jnp.broadcast_to(piece, (copies, BLOCK))
        out_ref[:, 8 * at + 6 : 8 * at + 8, :] = jnp.zeros((copies, 2, BLOCK), F32)


def spread(coords, beside, copies):
    return pl.pallas_call(
        spread_kernel,
        out_shape=shape_of(copies, 16, BLOCK),
        compiler_params=params(),
        cost_estimate=cost(1),
        name="spread",
    )(coords, beside)


def lookup_kernel(order_ref, table_ref, out_ref):
    mine = lax.axis_index("row")
    side = lax.axis_index("leaf") & 1
    numbers = order_ref[...]
    owner = numbers >> 8
    leaf_of = owner >> 2
    count = table_ref.shape[0]
    far = (leaf_of & 1) ^ side
    key = (2 * far + ((numbers >> 7) & 1)) * count + (leaf_of >> 1)
    key = jnp.where((owner & 3) == mine, key, -1)
    shape = (4 * count, numbers.shape[1])
    chosen = (lax.broadcasted_iota(jnp.int32, shape, 0) == key).astype(F32)
    lane = lax.broadcasted_iota(jnp.int32, (BLOCK, numbers.shape[1]), 0) == (numbers & 127)
    out_ref[...] = jnp.zeros_like(out_ref)
    for part in range(3):
        rows = (2 * part, 2 * part + 1, 8 + 2 * part, 9 + 2 * part)
        piece = jnp.concatenate([table_ref[:, row, :] for row in rows], axis=0)
        found = full_dot(piece.T, chosen)
        out_ref[part : part + 1, :] = jnp.sum(jnp.where(lane, found, 0.0), axis=0, keepdims=True)


def lookup(order_row, table):
    return pl.pallas_call(
        lookup_kernel,
        out_shape=jax.ShapeDtypeStruct((8, order_row.shape[1]), F32),
        compiler_params=params(),
        cost_estimate=cost(1.5),
        name="lookup",
    )(order_row, table)


def pivot_inverse(pivot, largest, products, between):
    scale = 2.0 / (largest + 1.0)
    cheb = (largest + 1.0) / (largest - 1.0)
    residual = eye() - scale * pivot
    total = eye()
    for step in range(products):
        total = total + (three_dot(residual, total) if step else residual)
        doubled = jnp.minimum(2.0 * cheb * cheb - 1.0, 1e18)
        grow, drop = (doubled + 1.0) / doubled, 1.0 / doubled
        scale = scale * grow
        cheb = doubled
        if step + 1 < products:
            residual = grow * three_dot(residual, residual) - drop * eye()
        for piece in between[step::products]:
            piece()
    return scale * total


def turn(rhs_ref, turned_ref, at):
    core = lax.axis_index("row") & 1
    for level in range(turned_ref.shape[0] // HALF):
        turned = rhs_ref[at, cols(level)].T
        half = jnp.where(core == 0, turned[:HALF], turned[HALF:])
        turned_ref[level * HALF : (level + 1) * HALF, at] = half


def eliminate_any(mat_ref, rhs_ref, sol_ref, own_x_ref, turned_ref, held, right_ref, largest):
    blocks = mat_ref.shape[0] // BLOCK

    def place(block):
        return pl.ds(pl.multiple_of(block * BLOCK, BLOCK), BLOCK)

    def product(_, carry):
        scale, cheb = carry
        doubled = jnp.minimum(2.0 * cheb * cheb - 1.0, 1e18)
        grow = (doubled + 1.0) / doubled
        held[1] = held[1] + full_dot(held[0], held[1])
        held[0] = grow * full_dot(held[0], held[0]) - eye() / doubled
        return scale * grow, doubled

    def step(block, _):
        at = place(block)
        held[0] = eye() - 2.0 / (largest + 1.0) * mat_ref[at, at]
        held[1] = eye()
        scale = lax.fori_loop(
            0, MANY, product, (2.0 / (largest + 1.0), (largest + 1.0) / (largest - 1.0))
        )[0]
        held[1] = scale * held[1]
        solved = full_dot(held[1], rhs_ref[at, :])
        sol_ref[at, :] = solved
        right = full_dot(held[1], mat_ref[at, :])

        @pl.when(block == blocks - 2)
        def _():
            right_ref[...] = right[:, cols(blocks - 1)]

        def below(index, _):
            row = place(index)
            left = mat_ref[row, at]
            mat_ref[row, :] -= full_dot(left, right)
            rhs_ref[row, :] -= full_dot(left, solved)
            return 0

        lax.fori_loop(block + 1, blocks, below, 0)
        turn(rhs_ref, turned_ref, at)
        return 0

    lax.fori_loop(0, blocks, step, 0)
    last = sol_ref[cols(blocks - 1), :]
    own_x_ref[cols(1), :] = last
    own_x_ref[cols(0), :] = sol_ref[cols(blocks - 2), :] - full_dot(right_ref[...], last)


def eliminate(mat_ref, rhs_ref, sol_ref, own_x_ref, turned_ref, largest, between):
    blocks = mat_ref.shape[0] // BLOCK
    pivot = mat_ref[cols(0), cols(0)]
    right = None

    for block in range(blocks):
        inverse = pivot_inverse(pivot, largest[block], FEW, between)
        after = blocks - block - 1
        solved = three_dot(inverse, rhs_ref[cols(block), :])
        sol_ref[cols(block), :] = solved
        if after == 0:
            break
        right = three_dot(inverse, mat_ref[cols(block), cols(block + 1, after)])
        down = mat_ref[cols(block + 1, after), cols(block)]
        pivot = mat_ref[cols(block + 1), cols(block + 1)] - three_dot(
            down[:BLOCK], right[:, :BLOCK]
        )
        high, low = split(down)
        left = jnp.concatenate([high, high, low], axis=1)
        high, low = split(right)
        mat_right = jnp.concatenate([high, low, high], axis=0)
        high, low = split(solved)
        rhs_right = jnp.concatenate([high, low, high], axis=0)

        def piece(index, block=block, left=left, mat_right=mat_right, rhs_right=rhs_right):
            row = cols(block + 1 + index)
            part = left[cols(index)]
            mat_ref[row, cols(block + 1, blocks - block - 1)] -= half_dot(part, mat_right)
            rhs_ref[row, :] -= half_dot(part, rhs_right)

        between = [functools.partial(piece, index) for index in range(after)]
        between.append(functools.partial(turn, rhs_ref, turned_ref, cols(block)))
    turn(rhs_ref, turned_ref, cols(blocks - 1))
    own_x_ref[cols(1), :] = solved
    own_x_ref[cols(0), :] = sol_ref[cols(blocks - 2), :] - full_dot(right, solved)


def leaf_kernel(
    own_ref, core_ref, chip_ref, far_ref, *refs, levels, scales
):
    basis_refs, target_refs = refs[:4], refs[4:8]
    first_ref, next_ref, soon_ref, rest_ref, own_x_ref = refs[8:13]
    mat_ref, rhs_ref, sol_ref, turned_ref, held_ref, right_ref, points_ref = refs[13:20]
    size = mat_ref.shape[0]
    blocks = size // BLOCK
    piece = size // 4
    width = rhs_ref.shape[1]
    pieces = []
    for spot in range(4):
        total = own_ref[:, spot * piece : (spot + 1) * piece]
        for mask, ref in ((1, core_ref), (2, chip_ref), (3, far_ref)):
            other = spot ^ mask
            total = total + ref[:, other * piece : (other + 1) * piece]
        pieces.append(total)
    points = jnp.concatenate(pieces, axis=1)
    for spot in range(4):
        rows = slice(spot * piece, (spot + 1) * piece)
        for level in range(levels):
            rhs_ref[rows, cols(level)] = basis_refs[spot][level] * scales[level]
        rhs_ref[rows, cols(levels)] = target_refs[spot][...]
    def kernel_rows(turned, at):
        squared = jnp.zeros((BLOCK, at.stop - at.start), F32)
        for part in range(3):
            offset = turned[:, part : part + 1] - points[part : part + 1, at]
            squared = squared + offset * offset
        return jnp.exp(squared * (-0.5 / (LENGTH_SCALE * LENGTH_SCALE)))

    largest, turned_points = [], []
    for block in range(blocks):
        turned_points.append(points[:, cols(block)].T)
        points_ref[cols(block), :] = turned_points[block]
        value = kernel_rows(turned_points[block], cols(block)) + NOISE_VAR * eye()
        mat_ref[cols(block), cols(block)] = value
        sums = jnp.sum(value, axis=0, keepdims=True)
        largest.append(jnp.max(sums, axis=1, keepdims=True) + 0.01)

    def build(block):
        for at in (slice(0, block * BLOCK), slice((block + 1) * BLOCK, size)):
            if at.stop > at.start:
                mat_ref[cols(block), at] = kernel_rows(turned_points[block], at)

    def build_any(block, _):
        at = pl.ds(pl.multiple_of(block * BLOCK, BLOCK), BLOCK)
        diagonal = mat_ref[at, at]
        mat_ref[at, :] = kernel_rows(points_ref[at, :], slice(0, size))
        mat_ref[at, at] = diagonal
        return 0

    bound = largest[0]
    for value in largest[1:]:
        bound = jnp.maximum(bound, value)
    small = jnp.max(bound) < FEW_LIMIT
    rows = [functools.partial(build, block) for block in range(blocks)]

    @pl.when(small)
    def _():
        eliminate(mat_ref, rhs_ref, sol_ref, own_x_ref, turned_ref, largest, rows)

    @pl.when(jnp.logical_not(small))
    def _():
        lax.fori_loop(0, blocks, build_any, 0)
        eliminate_any(
            mat_ref, rhs_ref, sol_ref, own_x_ref, turned_ref, held_ref, right_ref, bound
        )

    high, low = split(sol_ref[...])
    left_high, left_low = split(turned_ref[...])
    chunks = []
    for at in range(0, levels + 1, 2):
        rows = HALF * min(levels, at + 2)
        here = cols(at, min(2, levels + 1 - at))
        both = half_dot(
            jnp.concatenate([left_high[:rows], left_low[:rows]], axis=0), high[:, here]
        )
        chunks.append(both[:rows] + (both[rows:] + half_dot(left_high[:rows], low[:, here])))

    start = 0
    for level in range(levels):
        mine = slice(level * HALF, (level + 1) * HALF)
        value = jnp.concatenate(
            [chunks[level // 2][mine, (level % 2) * BLOCK :]]
            + [chunk[mine] for chunk in chunks[level // 2 + 1 :]],
            axis=1,
        )
        if level == 0:
            first_ref[...] = value
        elif level == 1:
            next_ref[...] = value
        elif level == 2:
            soon_ref[...] = value
        else:
            rest_ref[:, start : start + value.shape[1]] = value
            start += value.shape[1]


def rest_width(level, levels):
    return sum((levels + 1 - row) * BLOCK for row in range(level + 3, levels))


def shape_of(*shape):
    return jax.ShapeDtypeStruct(shape, F32)


def leaf(parts, bases, targets, scales):
    levels = len(scales)
    size = parts[0].shape[1]
    width = (levels + 1) * BLOCK
    return pl.pallas_call(
        functools.partial(leaf_kernel, levels=levels, scales=scales),
        out_shape=[
            shape_of(HALF, width),
            shape_of(HALF, width - BLOCK),
            shape_of(HALF, width - 2 * BLOCK),
            shape_of(HALF, rest_width(0, levels)),
            shape_of(2 * BLOCK, width),
        ],
        scratch_shapes=[
            pltpu.VMEM((size, size), F32),
            pltpu.VMEM((size, width), F32),
            pltpu.VMEM((size, width), F32),
            pltpu.VMEM((levels * HALF, size), F32),
            pltpu.VMEM((2, BLOCK, BLOCK), F32),
            pltpu.VMEM((BLOCK, BLOCK), F32),
            pltpu.VMEM((size, 8), F32),
        ],
        compiler_params=params(),
        cost_estimate=cost(30),
        name="leaf",
    )(*parts, *bases, *targets)


def whole(target_ref, mine_ref, other_ref):
    core = lax.axis_index("row") & 1
    target_ref[pl.ds(pl.multiple_of(core * HALF, HALF), HALF), :] = mine_ref[...]
    target_ref[pl.ds(pl.multiple_of((1 - core) * HALF, HALF), HALF), :] = other_ref[...]


def coefficients(own_ref, sib_ref, held):
    own_gram, sib_gram = own_ref[:, :BLOCK], sib_ref[:, :BLOCK]
    own_proj, sib_proj = own_ref[:, BLOCK:], sib_ref[:, BLOCK:]
    power = full_dot(own_gram, sib_gram)
    residual = own_proj - full_dot(own_gram, sib_proj)
    total = eye() + power
    power = full_dot(power, power)
    total = total + full_dot(power, total)
    power = full_dot(power, power)

    def norm(value):
        return jnp.max(jnp.sum(jnp.abs(value), axis=0, keepdims=True))

    held[0], held[1] = power, total + full_dot(power, total)

    def more(carry):
        return jnp.logical_and(carry[0] * carry[0] > ROUNDING, carry[1] < 40)

    def once(carry):
        power = full_dot(held[0], held[0])
        held[0] = power
        held[1] += full_dot(power, held[1])
        return norm(power), carry[1] + 1

    lax.while_loop(more, once, (norm(power), 0))
    sib_z = full_dot(held[1], residual)
    return sib_proj - full_dot(sib_gram, sib_z), sib_z


def level_kernel(*refs):
    own_mine_ref, own_other_ref, mine_ref, other_ref = refs[:4]
    own_ref, sib_ref, own_z_ref, sib_z_ref, held_ref = refs[4:]
    whole(own_ref, own_mine_ref, own_other_ref)
    whole(sib_ref, mine_ref, other_ref)
    own_z_ref[...], sib_z_ref[...] = coefficients(own_ref, sib_ref, held_ref)


def level_step(own_mine, own_other, mine, other):
    width = mine.shape[1]
    return pl.pallas_call(
        level_kernel,
        out_shape=[shape_of(BLOCK, width)] * 2 + [shape_of(BLOCK, width - BLOCK)] * 2,
        scratch_shapes=[pltpu.VMEM((2, BLOCK, BLOCK), F32)],
        compiler_params=params(),
        cost_estimate=cost(2),
        name="level",
    )(own_mine, own_other, mine, other)


def half_turned(own_ref, sib_ref, at):
    core = lax.axis_index("row") & 1
    turned = jnp.concatenate([own_ref[:, at].T, sib_ref[:, at].T], axis=1)
    return jnp.where(core == 0, turned[:HALF], turned[HALF:])


def parent_rows(refs, rest_ref, sib_rest_ref, rows, level, levels):
    own_ref, sib_ref, own_z_ref, sib_z_ref = refs
    both_z = jnp.concatenate([own_z_ref[...], sib_z_ref[...]], axis=0)
    start = 0
    for row in rows:
        span = (levels + 1 - row) * BLOCK
        here = slice(start, start + span)
        left = half_turned(own_ref, sib_ref, cols(row - level))
        yield (rest_ref[:, here] + sib_rest_ref[:, here]) - full_dot(
            left, both_z[:, (row - level - 1) * BLOCK :]
        )
        start += span


def row_kernel(*refs, row, level, levels, with_current):
    sums = parent_rows(refs[:4], refs[4], refs[5], [row], level, levels)
    if with_current:
        x_ref, out_ref, x_out_ref = refs[6:]
        x_out_ref[...] = x_ref[:, BLOCK:] - full_dot(x_ref[:, :BLOCK], refs[2][...])
    else:
        out_ref = refs[6]
    out_ref[...] = next(sums)


def row_step(whole_rows, mine, sib, row, level, levels, current=None):
    out_shape = [shape_of(*mine.shape)]
    operands = [*whole_rows, mine, sib]
    if current is not None:
        operands.append(current)
        out_shape.append(shape_of(current.shape[0], current.shape[1] - BLOCK))
    return pl.pallas_call(
        functools.partial(
            row_kernel, row=row, level=level, levels=levels, with_current=current is not None
        ),
        out_shape=out_shape,
        compiler_params=params(),
        cost_estimate=cost(1),
        name="row",
    )(*operands)


def rest_kernel(*refs, level, levels):
    x_ref, rest_ref, sib_rest_ref, x_out_ref, soon_ref = refs[4:9]
    rows = range(level + 3, levels)
    start = 0
    for row, value in zip(rows, parent_rows(refs[:4], rest_ref, sib_rest_ref, rows, level, levels)):
        if row == level + 3:
            soon_ref[...] = value
        else:
            refs[9][:, start : start + value.shape[1]] = value
            start += value.shape[1]
    x_out_ref[...] = x_ref[:, BLOCK:] - full_dot(x_ref[:, :BLOCK], refs[2][...])


def rest_step(whole_rows, current, rest, sib_rest, level, levels):
    out_shape = [
        shape_of(current.shape[0], current.shape[1] - BLOCK),
        shape_of(HALF, (levels - level - 2) * BLOCK),
    ]
    after = rest_width(level + 1, levels)
    if after:
        out_shape.append(shape_of(HALF, after))
    return pl.pallas_call(
        functools.partial(rest_kernel, level=level, levels=levels),
        out_shape=out_shape,
        compiler_params=params(),
        cost_estimate=cost(2),
        name="rest",
    )(*whole_rows, current, rest, sib_rest)


def final_kernel(*refs):
    own_mine_ref, own_other_ref, mine_ref, other_ref, x_ref, before_z_ref, out_ref = refs[:7]
    own_ref, sib_ref, held_ref = refs[7:]
    whole(own_ref, own_mine_ref, own_other_ref)
    whole(sib_ref, mine_ref, other_ref)
    current = x_ref[:, BLOCK:] - full_dot(x_ref[:, :BLOCK], before_z_ref[...])
    own_z, _ = coefficients(own_ref, sib_ref, held_ref)
    out_ref[...] = current[:, BLOCK:] - full_dot(current[:, :BLOCK], own_z)


def final_step(own_mine, own_other, mine, other, current, before_z):
    whole_row = pltpu.VMEM((BLOCK, mine.shape[1]), F32)
    return pl.pallas_call(
        final_kernel,
        out_shape=shape_of(current.shape[0], BLOCK),
        scratch_shapes=[whole_row, whole_row, pltpu.VMEM((2, BLOCK, BLOCK), F32)],
        compiler_params=params(),
        cost_estimate=cost(2),
        name="final",
    )(own_mine, own_other, mine, other, current, before_z)


PARTNERS = (4 | 2, 8, 16 | 8, 32, 64, 128 | 64 | 32)


def on_device(coords, order, targets, bases):
    levels = bases.shape[0]
    rows = targets.shape[0]
    leaf_size = rows * lax.axis_size("row")
    scales = tuple(float((leaf_size * 2**level) ** (-0.5)) for level in range(levels))
    orders = [order] + [swap(order, mask) for mask in (1, 2, 3)]
    beside = swap(coords, 4)
    half = lax.axis_size("leaf") // 2
    groups = [[2 * index + side for index in range(half)] for side in range(2)]
    beside, sent_bases, sent_targets, *orders = lax.optimization_barrier(
        (beside, bases, targets, *orders)
    )
    chip_bases, chip_targets = swap(sent_bases, 2), swap(sent_targets, 2)
    table = lax.all_to_all(
        spread(coords, beside, half), "leaf", 0, 0, axis_index_groups=groups, tiled=True
    )
    chip_bases, chip_targets, _ = lax.optimization_barrier((chip_bases, chip_targets, table))
    order_row = jnp.concatenate(orders[::-1]).reshape(1, leaf_size)
    part = lookup(order_row, table)
    parts = [part] + [swap(part, mask) for mask in (1, 2, 3)]
    all_bases = [swap(chip_bases, 1), chip_bases, swap(bases, 1), bases]
    all_targets = [swap(chip_targets, 1), chip_targets, swap(targets, 1), targets]
    own, coming, soon, rest, current = leaf(parts, all_bases, all_targets, scales)
    for level in range(levels):
        mask = PARTNERS[level]
        mine = swap(own, mask)
        own_other = swap(own, 1)
        other = swap(mine, 1)
        if level + 1 == levels:
            return final_step(own, own_other, mine, other, current, own_z)
        coming, _ = lax.optimization_barrier((coming, mine))
        sib_coming = swap(coming, mask)
        whole_rows = level_step(own, own_other, mine, other)
        own_z = whole_rows[2]
        own = row_step(whole_rows, coming, sib_coming, level + 1, level, levels)[0]
        if level + 2 == levels:
            continue
        soon, _ = lax.optimization_barrier((soon, own))
        sib_soon = swap(soon, mask)
        if level + 3 == levels:
            coming, current = row_step(
                whole_rows, soon, sib_soon, level + 2, level, levels, current
            )
            continue
        coming = row_step(whole_rows, soon, sib_soon, level + 2, level, levels)[0]
        rest, _ = lax.optimization_barrier((rest, coming))
        sib_rest = swap(rest, mask)
        sib_rest, _ = lax.optimization_barrier((sib_rest, coming))
        new = rest_step(whole_rows, current, rest, sib_rest, level, levels)
        current, soon = new[:2]
        rest = new[2] if len(new) > 2 else None


def solution(mesh):
    return jax.shard_map(
        on_device,
        mesh=mesh,
        in_specs=(
            P(None, AXES),
            P(AXES),
            P(AXES, None),
            P(None, AXES, None),
        ),
        out_specs=P(AXES, None),
        check_vma=False,
    )
```

```python
import functools

import jax
import jax.numpy as jnp
from jax import lax
from jax.experimental import pallas as pl
from jax.experimental.pallas import tpu as pltpu
from jax.sharding import PartitionSpec as P

LENGTH_SCALE = 0.1
NOISE_VAR = 1.0
BLOCK = 128
HALF = 64
ROUNDING = 3e-8
FEW, FEW_LIMIT, MANY = 5, 12.0, 7
AXES = ("leaf", "row")
F32 = jnp.float32


def params():
    return pltpu.CompilerParams(vmem_limit_bytes=48 * 1024 * 1024)


def cost(microseconds):
    return pl.CostEstimate(
        flops=int(microseconds * 1.15e9),
        bytes_accessed=int(microseconds * 3.6e6),
        transcendentals=0,
    )


def swap(value, mask):
    count = lax.axis_size(AXES)
    return lax.ppermute(value, AXES, [(index, index ^ mask) for index in range(count)])


def split(value):
    high = value.astype(jnp.bfloat16)
    return high, (value - high.astype(F32)).astype(jnp.bfloat16)


def full_dot(left, right):
    return jnp.dot(left, right, preferred_element_type=F32, precision=lax.Precision.HIGHEST)


def half_dot(left, right):
    return jnp.dot(left, right, preferred_element_type=F32)


def three_dot(left, right):
    high, low = split(left)
    right_high, right_low = split(right)
    return half_dot(
        jnp.concatenate([high, high, low], axis=1),
        jnp.concatenate([right_high, right_low, right_high], axis=0),
    )


def eye():
    rows = lax.broadcasted_iota(jnp.int32, (BLOCK, BLOCK), 0)
    cols = lax.broadcasted_iota(jnp.int32, (BLOCK, BLOCK), 1)
    return (rows == cols).astype(F32)


def cols(index, count=1):
    return slice(index * BLOCK, (index + count) * BLOCK)


def spread_kernel(coords_ref, beside_ref, out_ref):
    copies = out_ref.shape[0]
    for at, ref in enumerate((coords_ref, beside_ref)):
        for row in range(6):
            piece = ref[row // 2 : row // 2 + 1, cols(row % 2)]
            out_ref[:, 8 * at + row, :] = jnp.broadcast_to(piece, (copies, BLOCK))
        out_ref[:, 8 * at + 6 : 8 * at + 8, :] = jnp.zeros((copies, 2, BLOCK), F32)


def spread(coords, beside, copies):
    return pl.pallas_call(
        spread_kernel,
        out_shape=shape_of(copies, 16, BLOCK),
        compiler_params=params(),
        cost_estimate=cost(0.1),
        name="spread",
    )(coords, beside)


def lookup_kernel(order_ref, table_ref, out_ref):
    mine = lax.axis_index("row")
    side = lax.axis_index("leaf") & 1
    numbers = order_ref[...]
    owner = numbers >> 8
    leaf_of = owner >> 2
    count = table_ref.shape[0]
    far = (leaf_of & 1) ^ side
    key = (2 * far + ((numbers >> 7) & 1)) * count + (leaf_of >> 1)
    key = jnp.where((owner & 3) == mine, key, -1)
    shape = (4 * count, numbers.shape[1])
    chosen = (lax.broadcasted_iota(jnp.int32, shape, 0) == key).astype(F32)
    lane = lax.broadcasted_iota(jnp.int32, (BLOCK, numbers.shape[1]), 0) == (numbers & 127)
    out_ref[...] = jnp.zeros_like(out_ref)
    for part in range(3):
        rows = (2 * part, 2 * part + 1, 8 + 2 * part, 9 + 2 * part)
        piece = jnp.concatenate([table_ref[:, row, :] for row in rows], axis=0)
        found = full_dot(piece.T, chosen)
        out_ref[part : part + 1, :] = jnp.sum(jnp.where(lane, found, 0.0), axis=0, keepdims=True)


def lookup(order_row, table):
    return pl.pallas_call(
        lookup_kernel,
        out_shape=jax.ShapeDtypeStruct((8, order_row.shape[1]), F32),
        compiler_params=params(),
        cost_estimate=cost(1.5),
        name="lookup",
    )(order_row, table)


def pivot_inverse(pivot, largest, products, between):
    scale = 2.0 / (largest + 1.0)
    cheb = (largest + 1.0) / (largest - 1.0)
    residual = eye() - scale * pivot
    total = eye()
    for step in range(products):
        total = total + (three_dot(residual, total) if step else residual)
        doubled = jnp.minimum(2.0 * cheb * cheb - 1.0, 1e18)
        grow, drop = (doubled + 1.0) / doubled, 1.0 / doubled
        scale = scale * grow
        cheb = doubled
        if step + 1 < products:
            residual = grow * three_dot(residual, residual) - drop * eye()
        for piece in between[step::products]:
            piece()
    return scale * total


def turn(rhs_ref, turned_ref, at):
    core = lax.axis_index("row") & 1
    for level in range(turned_ref.shape[0] // HALF):
        turned = rhs_ref[at, cols(level)].T
        half = jnp.where(core == 0, turned[:HALF], turned[HALF:])
        turned_ref[level * HALF : (level + 1) * HALF, at] = half


def eliminate_any(mat_ref, rhs_ref, sol_ref, own_x_ref, turned_ref, held, right_ref, largest):
    blocks = mat_ref.shape[0] // BLOCK

    def place(block):
        return pl.ds(pl.multiple_of(block * BLOCK, BLOCK), BLOCK)

    def product(_, carry):
        scale, cheb = carry
        doubled = jnp.minimum(2.0 * cheb * cheb - 1.0, 1e18)
        grow = (doubled + 1.0) / doubled
        held[1] = held[1] + full_dot(held[0], held[1])
        held[0] = grow * full_dot(held[0], held[0]) - eye() / doubled
        return scale * grow, doubled

    def step(block, _):
        at = place(block)
        held[0] = eye() - 2.0 / (largest + 1.0) * mat_ref[at, at]
        held[1] = eye()
        scale = lax.fori_loop(
            0, MANY, product, (2.0 / (largest + 1.0), (largest + 1.0) / (largest - 1.0))
        )[0]
        held[1] = scale * held[1]
        solved = full_dot(held[1], rhs_ref[at, :])
        sol_ref[at, :] = solved
        right = full_dot(held[1], mat_ref[at, :])

        @pl.when(block == blocks - 2)
        def _():
            right_ref[...] = right[:, cols(blocks - 1)]

        def below(index, _):
            row = place(index)
            left = mat_ref[row, at]
            mat_ref[row, :] -= full_dot(left, right)
            rhs_ref[row, :] -= full_dot(left, solved)
            return 0

        lax.fori_loop(block + 1, blocks, below, 0)
        turn(rhs_ref, turned_ref, at)
        return 0

    lax.fori_loop(0, blocks, step, 0)
    last = sol_ref[cols(blocks - 1), :]
    own_x_ref[cols(1), :] = last
    own_x_ref[cols(0), :] = sol_ref[cols(blocks - 2), :] - full_dot(right_ref[...], last)


def eliminate(mat_ref, rhs_ref, sol_ref, own_x_ref, turned_ref, largest, between):
    blocks = mat_ref.shape[0] // BLOCK
    pivot = mat_ref[cols(0), cols(0)]
    right = None

    for block in range(blocks):
        inverse = pivot_inverse(pivot, largest[block], FEW, between)
        after = blocks - block - 1
        solved = three_dot(inverse, rhs_ref[cols(block), :])
        sol_ref[cols(block), :] = solved
        if after == 0:
            break
        right = three_dot(inverse, mat_ref[cols(block), cols(block + 1, after)])
        down = mat_ref[cols(block + 1, after), cols(block)]
        pivot = mat_ref[cols(block + 1), cols(block + 1)] - three_dot(
            down[:BLOCK], right[:, :BLOCK]
        )
        high, low = split(down)
        left = jnp.concatenate([high, high, low], axis=1)
        high, low = split(right)
        mat_right = jnp.concatenate([high, low, high], axis=0)
        high, low = split(solved)
        rhs_right = jnp.concatenate([high, low, high], axis=0)

        def piece(index, block=block, left=left, mat_right=mat_right, rhs_right=rhs_right):
            row = cols(block + 1 + index)
            part = left[cols(index)]
            mat_ref[row, cols(block + 1, blocks - block - 1)] -= half_dot(part, mat_right)
            rhs_ref[row, :] -= half_dot(part, rhs_right)

        between = [functools.partial(piece, index) for index in range(after)]
        between.append(functools.partial(turn, rhs_ref, turned_ref, cols(block)))
    turn(rhs_ref, turned_ref, cols(blocks - 1))
    own_x_ref[cols(1), :] = solved
    own_x_ref[cols(0), :] = sol_ref[cols(blocks - 2), :] - full_dot(right, solved)


def leaf_kernel(
    own_ref, core_ref, chip_ref, far_ref, *refs, levels, scales
):
    basis_refs, target_refs = refs[:4], refs[4:8]
    first_ref, next_ref, soon_ref, rest_ref, own_x_ref = refs[8:13]
    mat_ref, rhs_ref, sol_ref, turned_ref, held_ref, right_ref, points_ref = refs[13:20]
    size = mat_ref.shape[0]
    blocks = size // BLOCK
    piece = size // 4
    width = rhs_ref.shape[1]
    pieces = []
    for spot in range(4):
        total = own_ref[:, spot * piece : (spot + 1) * piece]
        for mask, ref in ((1, core_ref), (2, chip_ref), (3, far_ref)):
            other = spot ^ mask
            total = total + ref[:, other * piece : (other + 1) * piece]
        pieces.append(total)
    points = jnp.concatenate(pieces, axis=1)
    for spot in range(4):
        rows = slice(spot * piece, (spot + 1) * piece)
        for level in range(levels):
            rhs_ref[rows, cols(level)] = basis_refs[spot][level] * scales[level]
        rhs_ref[rows, cols(levels)] = target_refs[spot][...]
    def kernel_rows(turned, at):
        squared = jnp.zeros((BLOCK, at.stop - at.start), F32)
        for part in range(3):
            offset = turned[:, part : part + 1] - points[part : part + 1, at]
            squared = squared + offset * offset
        return jnp.exp(squared * (-0.5 / (LENGTH_SCALE * LENGTH_SCALE)))

    largest, turned_points = [], []
    for block in range(blocks):
        turned_points.append(points[:, cols(block)].T)
        points_ref[cols(block), :] = turned_points[block]
        value = kernel_rows(turned_points[block], cols(block)) + NOISE_VAR * eye()
        mat_ref[cols(block), cols(block)] = value
        sums = jnp.sum(value, axis=0, keepdims=True)
        largest.append(jnp.max(sums, axis=1, keepdims=True) + 0.01)

    def build(block):
        for at in (slice(0, block * BLOCK), slice((block + 1) * BLOCK, size)):
            if at.stop > at.start:
                mat_ref[cols(block), at] = kernel_rows(turned_points[block], at)

    def build_any(block, _):
        at = pl.ds(pl.multiple_of(block * BLOCK, BLOCK), BLOCK)
        diagonal = mat_ref[at, at]
        mat_ref[at, :] = kernel_rows(points_ref[at, :], slice(0, size))
        mat_ref[at, at] = diagonal
        return 0

    bound = largest[0]
    for value in largest[1:]:
        bound = jnp.maximum(bound, value)
    small = jnp.max(bound) < FEW_LIMIT
    rows = [functools.partial(build, block) for block in range(blocks)]

    @pl.when(small)
    def _():
        eliminate(mat_ref, rhs_ref, sol_ref, own_x_ref, turned_ref, largest, rows)

    @pl.when(jnp.logical_not(small))
    def _():
        lax.fori_loop(0, blocks, build_any, 0)
        eliminate_any(
            mat_ref, rhs_ref, sol_ref, own_x_ref, turned_ref, held_ref, right_ref, bound
        )

    high, low = split(sol_ref[...])
    left_high, left_low = split(turned_ref[...])
    chunks = []
    for at in range(0, levels + 1, 2):
        rows = HALF * min(levels, at + 2)
        here = cols(at, min(2, levels + 1 - at))
        both = half_dot(
            jnp.concatenate([left_high[:rows], left_low[:rows]], axis=0), high[:, here]
        )
        chunks.append(both[:rows] + (both[rows:] + half_dot(left_high[:rows], low[:, here])))

    start = 0
    for level in range(levels):
        mine = slice(level * HALF, (level + 1) * HALF)
        value = jnp.concatenate(
            [chunks[level // 2][mine, (level % 2) * BLOCK :]]
            + [chunk[mine] for chunk in chunks[level // 2 + 1 :]],
            axis=1,
        )
        if level == 0:
            first_ref[...] = value
        elif level == 1:
            next_ref[...] = value
        elif level == 2:
            soon_ref[...] = value
        else:
            rest_ref[:, start : start + value.shape[1]] = value
            start += value.shape[1]


def rest_width(level, levels):
    return sum((levels + 1 - row) * BLOCK for row in range(level + 3, levels))


def shape_of(*shape):
    return jax.ShapeDtypeStruct(shape, F32)


def leaf(parts, bases, targets, scales):
    levels = len(scales)
    size = parts[0].shape[1]
    width = (levels + 1) * BLOCK
    return pl.pallas_call(
        functools.partial(leaf_kernel, levels=levels, scales=scales),
        out_shape=[
            shape_of(HALF, width),
            shape_of(HALF, width - BLOCK),
            shape_of(HALF, width - 2 * BLOCK),
            shape_of(HALF, rest_width(0, levels)),
            shape_of(2 * BLOCK, width),
        ],
        scratch_shapes=[
            pltpu.VMEM((size, size), F32),
            pltpu.VMEM((size, width), F32),
            pltpu.VMEM((size, width), F32),
            pltpu.VMEM((levels * HALF, size), F32),
            pltpu.VMEM((2, BLOCK, BLOCK), F32),
            pltpu.VMEM((BLOCK, BLOCK), F32),
            pltpu.VMEM((size, 8), F32),
        ],
        compiler_params=params(),
        cost_estimate=cost(30),
        name="leaf",
    )(*parts, *bases, *targets)


def whole(target_ref, mine_ref, other_ref):
    core = lax.axis_index("row") & 1
    target_ref[pl.ds(pl.multiple_of(core * HALF, HALF), HALF), :] = mine_ref[...]
    target_ref[pl.ds(pl.multiple_of((1 - core) * HALF, HALF), HALF), :] = other_ref[...]


def coefficients(own_ref, sib_ref, held):
    own_gram, sib_gram = own_ref[:, :BLOCK], sib_ref[:, :BLOCK]
    own_proj, sib_proj = own_ref[:, BLOCK:], sib_ref[:, BLOCK:]
    power = full_dot(own_gram, sib_gram)
    residual = own_proj - full_dot(own_gram, sib_proj)
    total = eye() + power
    power = full_dot(power, power)
    total = total + full_dot(power, total)
    power = full_dot(power, power)

    def norm(value):
        return jnp.max(jnp.sum(jnp.abs(value), axis=0, keepdims=True))

    held[0], held[1] = power, total + full_dot(power, total)

    def more(carry):
        return jnp.logical_and(carry[0] * carry[0] > ROUNDING, carry[1] < 40)

    def once(carry):
        power = full_dot(held[0], held[0])
        held[0] = power
        held[1] += full_dot(power, held[1])
        return norm(power), carry[1] + 1

    lax.while_loop(more, once, (norm(power), 0))
    sib_z = full_dot(held[1], residual)
    return sib_proj - full_dot(sib_gram, sib_z), sib_z


def level_kernel(*refs):
    own_mine_ref, own_other_ref, mine_ref, other_ref = refs[:4]
    own_ref, sib_ref, own_z_ref, sib_z_ref, held_ref = refs[4:]
    whole(own_ref, own_mine_ref, own_other_ref)
    whole(sib_ref, mine_ref, other_ref)
    own_z_ref[...], sib_z_ref[...] = coefficients(own_ref, sib_ref, held_ref)


def level_step(own_mine, own_other, mine, other):
    width = mine.shape[1]
    return pl.pallas_call(
        level_kernel,
        out_shape=[shape_of(BLOCK, width)] * 2 + [shape_of(BLOCK, width - BLOCK)] * 2,
        scratch_shapes=[pltpu.VMEM((2, BLOCK, BLOCK), F32)],
        compiler_params=params(),
        cost_estimate=cost(0.2),
        name="level",
    )(own_mine, own_other, mine, other)


def half_turned(own_ref, sib_ref, at):
    core = lax.axis_index("row") & 1
    turned = jnp.concatenate([own_ref[:, at].T, sib_ref[:, at].T], axis=1)
    return jnp.where(core == 0, turned[:HALF], turned[HALF:])


def parent_rows(refs, rest_ref, sib_rest_ref, rows, level, levels):
    own_ref, sib_ref, own_z_ref, sib_z_ref = refs
    both_z = jnp.concatenate([own_z_ref[...], sib_z_ref[...]], axis=0)
    start = 0
    for row in rows:
        span = (levels + 1 - row) * BLOCK
        here = slice(start, start + span)
        left = half_turned(own_ref, sib_ref, cols(row - level))
        yield (rest_ref[:, here] + sib_rest_ref[:, here]) - full_dot(
            left, both_z[:, (row - level - 1) * BLOCK :]
        )
        start += span


def row_kernel(*refs, row, level, levels, with_current):
    sums = parent_rows(refs[:4], refs[4], refs[5], [row], level, levels)
    if with_current:
        x_ref, out_ref, x_out_ref = refs[6:]
        x_out_ref[...] = x_ref[:, BLOCK:] - full_dot(x_ref[:, :BLOCK], refs[2][...])
    else:
        out_ref = refs[6]
    out_ref[...] = next(sums)


def row_step(whole_rows, mine, sib, row, level, levels, current=None):
    out_shape = [shape_of(*mine.shape)]
    operands = [*whole_rows, mine, sib]
    if current is not None:
        operands.append(current)
        out_shape.append(shape_of(current.shape[0], current.shape[1] - BLOCK))
    return pl.pallas_call(
        functools.partial(
            row_kernel, row=row, level=level, levels=levels, with_current=current is not None
        ),
        out_shape=out_shape,
        compiler_params=params(),
        cost_estimate=cost(0.1),
        name="row",
    )(*operands)


def rest_kernel(*refs, level, levels):
    x_ref, rest_ref, sib_rest_ref, x_out_ref, soon_ref = refs[4:9]
    rows = range(level + 3, levels)
    start = 0
    for row, value in zip(rows, parent_rows(refs[:4], rest_ref, sib_rest_ref, rows, level, levels)):
        if row == level + 3:
            soon_ref[...] = value
        else:
            refs[9][:, start : start + value.shape[1]] = value
            start += value.shape[1]
    x_out_ref[...] = x_ref[:, BLOCK:] - full_dot(x_ref[:, :BLOCK], refs[2][...])


def rest_step(whole_rows, current, rest, sib_rest, level, levels):
    out_shape = [
        shape_of(current.shape[0], current.shape[1] - BLOCK),
        shape_of(HALF, (levels - level - 2) * BLOCK),
    ]
    after = rest_width(level + 1, levels)
    if after:
        out_shape.append(shape_of(HALF, after))
    return pl.pallas_call(
        functools.partial(rest_kernel, level=level, levels=levels),
        out_shape=out_shape,
        compiler_params=params(),
        cost_estimate=cost(0.2),
        name="rest",
    )(*whole_rows, current, rest, sib_rest)


def final_kernel(*refs):
    own_mine_ref, own_other_ref, mine_ref, other_ref, x_ref, before_z_ref, out_ref = refs[:7]
    own_ref, sib_ref, held_ref = refs[7:]
    whole(own_ref, own_mine_ref, own_other_ref)
    whole(sib_ref, mine_ref, other_ref)
    current = x_ref[:, BLOCK:] - full_dot(x_ref[:, :BLOCK], before_z_ref[...])
    own_z, _ = coefficients(own_ref, sib_ref, held_ref)
    out_ref[...] = current[:, BLOCK:] - full_dot(current[:, :BLOCK], own_z)


def final_step(own_mine, own_other, mine, other, current, before_z):
    whole_row = pltpu.VMEM((BLOCK, mine.shape[1]), F32)
    return pl.pallas_call(
        final_kernel,
        out_shape=shape_of(current.shape[0], BLOCK),
        scratch_shapes=[whole_row, whole_row, pltpu.VMEM((2, BLOCK, BLOCK), F32)],
        compiler_params=params(),
        cost_estimate=cost(0.2),
        name="final",
    )(own_mine, own_other, mine, other, current, before_z)


PARTNERS = (4 | 2, 8, 16 | 8, 32, 64, 128 | 64 | 32)


def on_device(coords, order, targets, bases):
    levels = bases.shape[0]
    rows = targets.shape[0]
    leaf_size = rows * lax.axis_size("row")
    scales = tuple(float((leaf_size * 2**level) ** (-0.5)) for level in range(levels))
    orders = [order] + [swap(order, mask) for mask in (1, 2, 3)]
    beside = swap(coords, 4)
    half = lax.axis_size("leaf") // 2
    groups = [[2 * index + side for index in range(half)] for side in range(2)]
    beside, sent_bases, sent_targets, *orders = lax.optimization_barrier(
        (beside, bases, targets, *orders)
    )
    chip_bases, chip_targets = swap(sent_bases, 2), swap(sent_targets, 2)
    table = lax.all_to_all(
        spread(coords, beside, half), "leaf", 0, 0, axis_index_groups=groups, tiled=True
    )
    chip_bases, chip_targets, _ = lax.optimization_barrier((chip_bases, chip_targets, table))
    order_row = jnp.concatenate(orders[::-1]).reshape(1, leaf_size)
    part = lookup(order_row, table)
    parts = [part] + [swap(part, mask) for mask in (1, 2, 3)]
    all_bases = [swap(chip_bases, 1), chip_bases, swap(bases, 1), bases]
    all_targets = [swap(chip_targets, 1), chip_targets, swap(targets, 1), targets]
    own, coming, soon, rest, current = leaf(parts, all_bases, all_targets, scales)
    waiting = None
    for level in range(levels):
        mask = PARTNERS[level]
        mine = swap(own, mask)
        own_other = swap(own, 1)
        if level == 0:
            sib_coming = swap(coming, mask)
            mine, sib_coming = lax.optimization_barrier((mine, sib_coming))
        other = swap(mine, 1)
        if level + 1 == levels:
            return final_step(own, own_other, mine, other, current, own_z)
        if level:
            coming, _ = lax.optimization_barrier((coming, own_other))
            sib_coming = swap(coming, mask)
        whole_rows = level_step(own, own_other, mine, other)
        own_z = whole_rows[2]
        if waiting is not None:
            sib_rest, _ = lax.optimization_barrier((sib_rest, own_z))
            new = rest_step(waiting, current, rest, sib_rest, level - 1, levels)
            current, soon = new[:2]
            rest = new[2] if len(new) > 2 else None
            waiting = None
        if level + 2 < levels:
            soon, _ = lax.optimization_barrier((soon, mine))
            sib_soon = swap(soon, mask)
        if level + 3 < levels:
            rest, _ = lax.optimization_barrier((rest, own_z))
            sib_rest = swap(rest, mask)
            waiting = whole_rows
        own = row_step(whole_rows, coming, sib_coming, level + 1, level, levels)[0]
        if level + 2 < levels:
            sib_soon, _ = lax.optimization_barrier((sib_soon, own))
            with_current = None if waiting is not None else current
            new = row_step(whole_rows, soon, sib_soon, level + 2, level, levels, with_current)
            coming = new[0]
            if waiting is None:
                current = new[1]


def solution(mesh):
    return jax.shard_map(
        on_device,
        mesh=mesh,
        in_specs=(
            P(None, AXES),
            P(AXES),
            P(AXES, None),
            P(None, AXES, None),
        ),
        out_specs=P(AXES, None),
        check_vma=False,
    )
```

```python
import functools

import jax
import jax.numpy as jnp
from jax import lax
from jax.experimental import pallas as pl
from jax.experimental.pallas import tpu as pltpu
from jax.sharding import PartitionSpec as P

LENGTH_SCALE = 0.1
NOISE_VAR = 1.0
BLOCK = 128
HALF = 64
ROUNDING = 3e-8
FEW, FEW_LIMIT, MANY = 5, 12.0, 7
AXES = ("leaf", "row")
F32 = jnp.float32


def params():
    return pltpu.CompilerParams(vmem_limit_bytes=48 * 1024 * 1024)


def cost(microseconds):
    return pl.CostEstimate(
        flops=int(microseconds * 1.15e9),
        bytes_accessed=int(microseconds * 3.6e6),
        transcendentals=0,
    )


def swap(value, mask):
    count = lax.axis_size(AXES)
    return lax.ppermute(value, AXES, [(index, index ^ mask) for index in range(count)])


def split(value):
    high = value.astype(jnp.bfloat16)
    return high, (value - high.astype(F32)).astype(jnp.bfloat16)


def full_dot(left, right):
    return jnp.dot(left, right, preferred_element_type=F32, precision=lax.Precision.HIGHEST)


def half_dot(left, right):
    return jnp.dot(left, right, preferred_element_type=F32)


def three_dot(left, right):
    high, low = split(left)
    right_high, right_low = split(right)
    return half_dot(
        jnp.concatenate([high, high, low], axis=1),
        jnp.concatenate([right_high, right_low, right_high], axis=0),
    )


def eye():
    rows = lax.broadcasted_iota(jnp.int32, (BLOCK, BLOCK), 0)
    cols = lax.broadcasted_iota(jnp.int32, (BLOCK, BLOCK), 1)
    return (rows == cols).astype(F32)


def cols(index, count=1):
    return slice(index * BLOCK, (index + count) * BLOCK)


def spread_kernel(coords_ref, beside_ref, out_ref):
    copies = out_ref.shape[0]
    for at, ref in enumerate((coords_ref, beside_ref)):
        for row in range(6):
            piece = ref[row // 2 : row // 2 + 1, cols(row % 2)]
            out_ref[:, 8 * at + row, :] = jnp.broadcast_to(piece, (copies, BLOCK))
        out_ref[:, 8 * at + 6 : 8 * at + 8, :] = jnp.zeros((copies, 2, BLOCK), F32)


def spread(coords, beside, copies):
    return pl.pallas_call(
        spread_kernel,
        out_shape=shape_of(copies, 16, BLOCK),
        compiler_params=params(),
        cost_estimate=cost(0.1),
        name="spread",
    )(coords, beside)


def lookup_kernel(order_ref, table_ref, out_ref):
    mine = lax.axis_index("row")
    side = lax.axis_index("leaf") & 1
    numbers = order_ref[...]
    owner = numbers >> 8
    leaf_of = owner >> 2
    count = table_ref.shape[0]
    far = (leaf_of & 1) ^ side
    key = (2 * far + ((numbers >> 7) & 1)) * count + (leaf_of >> 1)
    key = jnp.where((owner & 3) == mine, key, -1)
    shape = (4 * count, numbers.shape[1])
    chosen = (lax.broadcasted_iota(jnp.int32, shape, 0) == key).astype(F32)
    lane = lax.broadcasted_iota(jnp.int32, (BLOCK, numbers.shape[1]), 0) == (numbers & 127)
    out_ref[...] = jnp.zeros_like(out_ref)
    for part in range(3):
        rows = (2 * part, 2 * part + 1, 8 + 2 * part, 9 + 2 * part)
        piece = jnp.concatenate([table_ref[:, row, :] for row in rows], axis=0)
        found = full_dot(piece.T, chosen)
        out_ref[part : part + 1, :] = jnp.sum(jnp.where(lane, found, 0.0), axis=0, keepdims=True)


def lookup(order_row, table):
    return pl.pallas_call(
        lookup_kernel,
        out_shape=jax.ShapeDtypeStruct((8, order_row.shape[1]), F32),
        compiler_params=params(),
        cost_estimate=cost(1.5),
        name="lookup",
    )(order_row, table)


def pivot_inverse(pivot, largest, products, between):
    scale = 2.0 / (largest + 1.0)
    cheb = (largest + 1.0) / (largest - 1.0)
    residual = eye() - scale * pivot
    total = eye()
    for step in range(products):
        total = total + (three_dot(residual, total) if step else residual)
        doubled = jnp.minimum(2.0 * cheb * cheb - 1.0, 1e18)
        grow, drop = (doubled + 1.0) / doubled, 1.0 / doubled
        scale = scale * grow
        cheb = doubled
        if step + 1 < products:
            residual = grow * three_dot(residual, residual) - drop * eye()
        for piece in between[step::products]:
            piece()
    return scale * total


def turn(rhs_ref, turned_ref, at):
    core = lax.axis_index("row") & 1
    for level in range(turned_ref.shape[0] // HALF):
        turned = rhs_ref[at, cols(level)].T
        half = jnp.where(core == 0, turned[:HALF], turned[HALF:])
        turned_ref[level * HALF : (level + 1) * HALF, at] = half


def eliminate_any(mat_ref, rhs_ref, sol_ref, own_x_ref, turned_ref, held, right_ref, largest):
    blocks = mat_ref.shape[0] // BLOCK

    def place(block):
        return pl.ds(pl.multiple_of(block * BLOCK, BLOCK), BLOCK)

    def product(_, carry):
        scale, cheb = carry
        doubled = jnp.minimum(2.0 * cheb * cheb - 1.0, 1e18)
        grow = (doubled + 1.0) / doubled
        held[1] = held[1] + full_dot(held[0], held[1])
        held[0] = grow * full_dot(held[0], held[0]) - eye() / doubled
        return scale * grow, doubled

    def step(block, _):
        at = place(block)
        held[0] = eye() - 2.0 / (largest + 1.0) * mat_ref[at, at]
        held[1] = eye()
        scale = lax.fori_loop(
            0, MANY, product, (2.0 / (largest + 1.0), (largest + 1.0) / (largest - 1.0))
        )[0]
        held[1] = scale * held[1]
        solved = full_dot(held[1], rhs_ref[at, :])
        sol_ref[at, :] = solved
        right = full_dot(held[1], mat_ref[at, :])

        @pl.when(block == blocks - 2)
        def _():
            right_ref[...] = right[:, cols(blocks - 1)]

        def below(index, _):
            row = place(index)
            left = mat_ref[row, at]
            mat_ref[row, :] -= full_dot(left, right)
            rhs_ref[row, :] -= full_dot(left, solved)
            return 0

        lax.fori_loop(block + 1, blocks, below, 0)
        turn(rhs_ref, turned_ref, at)
        return 0

    lax.fori_loop(0, blocks, step, 0)
    last = sol_ref[cols(blocks - 1), :]
    own_x_ref[cols(1), :] = last
    own_x_ref[cols(0), :] = sol_ref[cols(blocks - 2), :] - full_dot(right_ref[...], last)


def eliminate(mat_ref, rhs_ref, sol_ref, own_x_ref, turned_ref, largest, between):
    blocks = mat_ref.shape[0] // BLOCK
    pivot = mat_ref[cols(0), cols(0)]
    right = None

    for block in range(blocks):
        inverse = pivot_inverse(pivot, largest[block], FEW, between)
        after = blocks - block - 1
        solved = three_dot(inverse, rhs_ref[cols(block), :])
        sol_ref[cols(block), :] = solved
        if after == 0:
            break
        right = three_dot(inverse, mat_ref[cols(block), cols(block + 1, after)])
        down = mat_ref[cols(block + 1, after), cols(block)]
        pivot = mat_ref[cols(block + 1), cols(block + 1)] - three_dot(
            down[:BLOCK], right[:, :BLOCK]
        )
        high, low = split(down)
        left = jnp.concatenate([high, high, low], axis=1)
        high, low = split(right)
        mat_right = jnp.concatenate([high, low, high], axis=0)
        high, low = split(solved)
        rhs_right = jnp.concatenate([high, low, high], axis=0)

        def piece(index, block=block, left=left, mat_right=mat_right, rhs_right=rhs_right):
            row = cols(block + 1 + index)
            part = left[cols(index)]
            mat_ref[row, cols(block + 1, blocks - block - 1)] -= half_dot(part, mat_right)
            rhs_ref[row, :] -= half_dot(part, rhs_right)

        between = [functools.partial(piece, index) for index in range(after)]
        between.append(functools.partial(turn, rhs_ref, turned_ref, cols(block)))
    turn(rhs_ref, turned_ref, cols(blocks - 1))
    own_x_ref[cols(1), :] = solved
    own_x_ref[cols(0), :] = sol_ref[cols(blocks - 2), :] - three_dot(right, solved)


def leaf_kernel(
    own_ref, core_ref, chip_ref, far_ref, *refs, levels, scales
):
    basis_refs, target_refs = refs[:4], refs[4:8]
    first_ref, next_ref, soon_ref, rest_ref, own_x_ref = refs[8:13]
    mat_ref, rhs_ref, sol_ref, turned_ref, held_ref, right_ref, points_ref = refs[13:20]
    size = mat_ref.shape[0]
    blocks = size // BLOCK
    piece = size // 4
    width = rhs_ref.shape[1]
    pieces = []
    for spot in range(4):
        total = own_ref[:, spot * piece : (spot + 1) * piece]
        for mask, ref in ((1, core_ref), (2, chip_ref), (3, far_ref)):
            other = spot ^ mask
            total = total + ref[:, other * piece : (other + 1) * piece]
        pieces.append(total)
    points = jnp.concatenate(pieces, axis=1)
    for spot in range(4):
        rows = slice(spot * piece, (spot + 1) * piece)
        for level in range(levels):
            rhs_ref[rows, cols(level)] = basis_refs[spot][level] * scales[level]
        rhs_ref[rows, cols(levels)] = target_refs[spot][...]
    def kernel_rows(turned, at):
        squared = jnp.zeros((BLOCK, at.stop - at.start), F32)
        for part in range(3):
            offset = turned[:, part : part + 1] - points[part : part + 1, at]
            squared = squared + offset * offset
        return jnp.exp(squared * (-0.5 / (LENGTH_SCALE * LENGTH_SCALE)))

    largest, turned_points = [], []
    for block in range(blocks):
        turned_points.append(points[:, cols(block)].T)
        points_ref[cols(block), :] = turned_points[block]
        value = kernel_rows(turned_points[block], cols(block)) + NOISE_VAR * eye()
        mat_ref[cols(block), cols(block)] = value
        sums = jnp.sum(value, axis=0, keepdims=True)
        largest.append(jnp.max(sums, axis=1, keepdims=True) + 0.01)

    def build(block):
        for at in (slice(0, block * BLOCK), slice((block + 1) * BLOCK, size)):
            if at.stop > at.start:
                mat_ref[cols(block), at] = kernel_rows(turned_points[block], at)

    def build_any(block, _):
        at = pl.ds(pl.multiple_of(block * BLOCK, BLOCK), BLOCK)
        diagonal = mat_ref[at, at]
        mat_ref[at, :] = kernel_rows(points_ref[at, :], slice(0, size))
        mat_ref[at, at] = diagonal
        return 0

    bound = largest[0]
    for value in largest[1:]:
        bound = jnp.maximum(bound, value)
    small = jnp.max(bound) < FEW_LIMIT
    rows = [functools.partial(build, block) for block in range(blocks)]

    @pl.when(small)
    def _():
        eliminate(mat_ref, rhs_ref, sol_ref, own_x_ref, turned_ref, largest, rows)

    @pl.when(jnp.logical_not(small))
    def _():
        lax.fori_loop(0, blocks, build_any, 0)
        eliminate_any(
            mat_ref, rhs_ref, sol_ref, own_x_ref, turned_ref, held_ref, right_ref, bound
        )

    high, low = split(sol_ref[...])
    left_high, left_low = split(turned_ref[...])
    chunks = []
    for at in range(0, levels + 1, 2):
        rows = HALF * min(levels, at + 2)
        here = cols(at, min(2, levels + 1 - at))
        both = half_dot(
            jnp.concatenate([left_high[:rows], left_low[:rows]], axis=0), high[:, here]
        )
        chunks.append(both[:rows] + (both[rows:] + half_dot(left_high[:rows], low[:, here])))

    start = 0
    for level in range(levels):
        mine = slice(level * HALF, (level + 1) * HALF)
        value = jnp.concatenate(
            [chunks[level // 2][mine, (level % 2) * BLOCK :]]
            + [chunk[mine] for chunk in chunks[level // 2 + 1 :]],
            axis=1,
        )
        if level == 0:
            first_ref[...] = value
        elif level == 1:
            next_ref[...] = value
        elif level == 2:
            soon_ref[...] = value
        else:
            rest_ref[:, start : start + value.shape[1]] = value
            start += value.shape[1]


def rest_width(level, levels):
    return sum((levels + 1 - row) * BLOCK for row in range(level + 3, levels))


def shape_of(*shape):
    return jax.ShapeDtypeStruct(shape, F32)


def leaf(parts, bases, targets, scales):
    levels = len(scales)
    size = parts[0].shape[1]
    width = (levels + 1) * BLOCK
    return pl.pallas_call(
        functools.partial(leaf_kernel, levels=levels, scales=scales),
        out_shape=[
            shape_of(HALF, width),
            shape_of(HALF, width - BLOCK),
            shape_of(HALF, width - 2 * BLOCK),
            shape_of(HALF, rest_width(0, levels)),
            shape_of(2 * BLOCK, width),
        ],
        scratch_shapes=[
            pltpu.VMEM((size, size), F32),
            pltpu.VMEM((size, width), F32),
            pltpu.VMEM((size, width), F32),
            pltpu.VMEM((levels * HALF, size), F32),
            pltpu.VMEM((2, BLOCK, BLOCK), F32),
            pltpu.VMEM((BLOCK, BLOCK), F32),
            pltpu.VMEM((size, 8), F32),
        ],
        compiler_params=params(),
        cost_estimate=cost(30),
        name="leaf",
    )(*parts, *bases, *targets)


def whole(target_ref, mine_ref, other_ref):
    core = lax.axis_index("row") & 1
    target_ref[pl.ds(pl.multiple_of(core * HALF, HALF), HALF), :] = mine_ref[...]
    target_ref[pl.ds(pl.multiple_of((1 - core) * HALF, HALF), HALF), :] = other_ref[...]


def coefficients(own_ref, sib_ref, held):
    own_gram, sib_gram = own_ref[:, :BLOCK], sib_ref[:, :BLOCK]
    own_proj, sib_proj = own_ref[:, BLOCK:], sib_ref[:, BLOCK:]
    power = full_dot(own_gram, sib_gram)
    residual = own_proj - three_dot(own_gram, sib_proj)
    total = eye() + power
    power = full_dot(power, power)
    total = total + full_dot(power, total)
    power = full_dot(power, power)

    def norm(value):
        return jnp.max(jnp.sum(jnp.abs(value), axis=0, keepdims=True))

    held[0], held[1] = power, total + full_dot(power, total)

    def more(carry):
        return jnp.logical_and(carry[0] * carry[0] > ROUNDING, carry[1] < 40)

    def once(carry):
        power = full_dot(held[0], held[0])
        held[0] = power
        held[1] += full_dot(power, held[1])
        return norm(power), carry[1] + 1

    lax.while_loop(more, once, (norm(power), 0))
    sib_z = three_dot(held[1], residual)
    return sib_proj - three_dot(sib_gram, sib_z), sib_z


def level_kernel(*refs):
    own_mine_ref, own_other_ref, mine_ref, other_ref = refs[:4]
    own_ref, sib_ref, own_z_ref, sib_z_ref, held_ref = refs[4:]
    whole(own_ref, own_mine_ref, own_other_ref)
    whole(sib_ref, mine_ref, other_ref)
    own_z_ref[...], sib_z_ref[...] = coefficients(own_ref, sib_ref, held_ref)


def level_step(own_mine, own_other, mine, other):
    width = mine.shape[1]
    return pl.pallas_call(
        level_kernel,
        out_shape=[shape_of(BLOCK, width)] * 2 + [shape_of(BLOCK, width - BLOCK)] * 2,
        scratch_shapes=[pltpu.VMEM((2, BLOCK, BLOCK), F32)],
        compiler_params=params(),
        cost_estimate=cost(0.2),
        name="level",
    )(own_mine, own_other, mine, other)


def half_turned(own_ref, sib_ref, at):
    core = lax.axis_index("row") & 1
    turned = jnp.concatenate([own_ref[:, at].T, sib_ref[:, at].T], axis=1)
    return jnp.where(core == 0, turned[:HALF], turned[HALF:])


def parent_rows(refs, rest_ref, sib_rest_ref, rows, level, levels):
    own_ref, sib_ref, own_z_ref, sib_z_ref = refs
    both_z = jnp.concatenate([own_z_ref[...], sib_z_ref[...]], axis=0)
    start = 0
    for row in rows:
        span = (levels + 1 - row) * BLOCK
        here = slice(start, start + span)
        left = half_turned(own_ref, sib_ref, cols(row - level))
        yield (rest_ref[:, here] + sib_rest_ref[:, here]) - three_dot(
            left, both_z[:, (row - level - 1) * BLOCK :]
        )
        start += span


def row_kernel(*refs, row, level, levels, with_current):
    sums = parent_rows(refs[:4], refs[4], refs[5], [row], level, levels)
    if with_current:
        x_ref, out_ref, x_out_ref = refs[6:]
        x_out_ref[...] = x_ref[:, BLOCK:] - three_dot(x_ref[:, :BLOCK], refs[2][...])
    else:
        out_ref = refs[6]
    out_ref[...] = next(sums)


def row_step(whole_rows, mine, sib, row, level, levels, current=None):
    out_shape = [shape_of(*mine.shape)]
    operands = [*whole_rows, mine, sib]
    if current is not None:
        operands.append(current)
        out_shape.append(shape_of(current.shape[0], current.shape[1] - BLOCK))
    return pl.pallas_call(
        functools.partial(
            row_kernel, row=row, level=level, levels=levels, with_current=current is not None
        ),
        out_shape=out_shape,
        compiler_params=params(),
        cost_estimate=cost(0.1),
        name="row",
    )(*operands)


def rest_kernel(*refs, level, levels):
    x_ref, rest_ref, sib_rest_ref, x_out_ref, soon_ref = refs[4:9]
    rows = range(level + 3, levels)
    start = 0
    for row, value in zip(rows, parent_rows(refs[:4], rest_ref, sib_rest_ref, rows, level, levels)):
        if row == level + 3:
            soon_ref[...] = value
        else:
            refs[9][:, start : start + value.shape[1]] = value
            start += value.shape[1]
    x_out_ref[...] = x_ref[:, BLOCK:] - three_dot(x_ref[:, :BLOCK], refs[2][...])


def rest_step(whole_rows, current, rest, sib_rest, level, levels):
    out_shape = [
        shape_of(current.shape[0], current.shape[1] - BLOCK),
        shape_of(HALF, (levels - level - 2) * BLOCK),
    ]
    after = rest_width(level + 1, levels)
    if after:
        out_shape.append(shape_of(HALF, after))
    return pl.pallas_call(
        functools.partial(rest_kernel, level=level, levels=levels),
        out_shape=out_shape,
        compiler_params=params(),
        cost_estimate=cost(0.2),
        name="rest",
    )(*whole_rows, current, rest, sib_rest)


def final_kernel(*refs):
    own_mine_ref, own_other_ref, mine_ref, other_ref, x_ref, before_z_ref, out_ref = refs[:7]
    own_ref, sib_ref, held_ref = refs[7:]
    whole(own_ref, own_mine_ref, own_other_ref)
    whole(sib_ref, mine_ref, other_ref)
    current = x_ref[:, BLOCK:] - three_dot(x_ref[:, :BLOCK], before_z_ref[...])
    own_z, _ = coefficients(own_ref, sib_ref, held_ref)
    out_ref[...] = current[:, BLOCK:] - three_dot(current[:, :BLOCK], own_z)


def final_step(own_mine, own_other, mine, other, current, before_z):
    whole_row = pltpu.VMEM((BLOCK, mine.shape[1]), F32)
    return pl.pallas_call(
        final_kernel,
        out_shape=shape_of(current.shape[0], BLOCK),
        scratch_shapes=[whole_row, whole_row, pltpu.VMEM((2, BLOCK, BLOCK), F32)],
        compiler_params=params(),
        cost_estimate=cost(0.2),
        name="final",
    )(own_mine, own_other, mine, other, current, before_z)


PARTNERS = (4 | 2, 8, 16 | 8, 32, 64, 128 | 64 | 32)


def on_device(coords, order, targets, bases):
    levels = bases.shape[0]
    rows = targets.shape[0]
    leaf_size = rows * lax.axis_size("row")
    scales = tuple(float((leaf_size * 2**level) ** (-0.5)) for level in range(levels))
    orders = [order] + [swap(order, mask) for mask in (1, 2, 3)]
    beside = swap(coords, 4)
    half = lax.axis_size("leaf") // 2
    groups = [[2 * index + side for index in range(half)] for side in range(2)]
    beside, sent_bases, sent_targets, *orders = lax.optimization_barrier(
        (beside, bases, targets, *orders)
    )
    chip_bases, chip_targets = swap(sent_bases, 2), swap(sent_targets, 2)
    table = lax.all_to_all(
        spread(coords, beside, half), "leaf", 0, 0, axis_index_groups=groups, tiled=True
    )
    chip_bases, chip_targets, _ = lax.optimization_barrier((chip_bases, chip_targets, table))
    order_row = jnp.concatenate(orders[::-1]).reshape(1, leaf_size)
    part = lookup(order_row, table)
    parts = [part] + [swap(part, mask) for mask in (1, 2, 3)]
    all_bases = [swap(chip_bases, 1), chip_bases, swap(bases, 1), bases]
    all_targets = [swap(chip_targets, 1), chip_targets, swap(targets, 1), targets]
    own, coming, soon, rest, current = leaf(parts, all_bases, all_targets, scales)
    waiting = None
    for level in range(levels):
        mask = PARTNERS[level]
        mine = swap(own, mask)
        own_other = swap(own, 1)
        if level == 0:
            sib_coming = swap(coming, mask)
            mine, sib_coming = lax.optimization_barrier((mine, sib_coming))
        other = swap(mine, 1)
        if level + 1 == levels:
            return final_step(own, own_other, mine, other, current, own_z)
        if level:
            coming, _ = lax.optimization_barrier((coming, own_other))
            sib_coming = swap(coming, mask)
        whole_rows = level_step(own, own_other, mine, other)
        own_z = whole_rows[2]
        if waiting is not None:
            sib_rest, _ = lax.optimization_barrier((sib_rest, own_z))
            new = rest_step(waiting, current, rest, sib_rest, level - 1, levels)
            current, soon = new[:2]
            rest = new[2] if len(new) > 2 else None
            waiting = None
        if level + 2 < levels:
            soon, _ = lax.optimization_barrier((soon, mine))
            sib_soon = swap(soon, mask)
        if level + 3 < levels:
            rest, _ = lax.optimization_barrier((rest, own_z))
            sib_rest = swap(rest, mask)
            waiting = whole_rows
        own = row_step(whole_rows, coming, sib_coming, level + 1, level, levels)[0]
        if level + 2 < levels:
            sib_soon, _ = lax.optimization_barrier((sib_soon, own))
            with_current = None if waiting is not None else current
            new = row_step(whole_rows, soon, sib_soon, level + 2, level, levels, with_current)
            coming = new[0]
            if waiting is None:
                current = new[1]


def solution(mesh):
    return jax.shard_map(
        on_device,
        mesh=mesh,
        in_specs=(
            P(None, AXES),
            P(AXES),
            P(AXES, None),
            P(None, AXES, None),
        ),
        out_specs=P(AXES, None),
        check_vma=False,
    )
```

```python
import functools

import jax
import jax.numpy as jnp
from jax import lax
from jax.experimental import pallas as pl
from jax.experimental.pallas import tpu as pltpu
from jax.sharding import PartitionSpec as P

LENGTH_SCALE = 0.1
NOISE_VAR = 1.0
BLOCK = 128
HALF = 64
ROUNDING = 3e-8
FEW, FEW_LIMIT, MANY = 5, 12.0, 7
AXES = ("leaf", "row")
F32 = jnp.float32


def params():
    return pltpu.CompilerParams(vmem_limit_bytes=48 * 1024 * 1024)


def cost(microseconds):
    return pl.CostEstimate(
        flops=int(microseconds * 1.15e9),
        bytes_accessed=int(microseconds * 3.6e6),
        transcendentals=0,
    )


def swap(value, mask):
    count = lax.axis_size(AXES)
    return lax.ppermute(value, AXES, [(index, index ^ mask) for index in range(count)])


def split(value):
    high = value.astype(jnp.bfloat16)
    return high, (value - high.astype(F32)).astype(jnp.bfloat16)


def full_dot(left, right):
    return jnp.dot(left, right, preferred_element_type=F32, precision=lax.Precision.HIGHEST)


def half_dot(left, right):
    return jnp.dot(left, right, preferred_element_type=F32)


def three_dot(left, right):
    high, low = split(left)
    right_high, right_low = split(right)
    return half_dot(
        jnp.concatenate([high, high, low], axis=1),
        jnp.concatenate([right_high, right_low, right_high], axis=0),
    )


def eye():
    rows = lax.broadcasted_iota(jnp.int32, (BLOCK, BLOCK), 0)
    cols = lax.broadcasted_iota(jnp.int32, (BLOCK, BLOCK), 1)
    return (rows == cols).astype(F32)


def cols(index, count=1):
    return slice(index * BLOCK, (index + count) * BLOCK)


def spread_kernel(coords_ref, beside_ref, out_ref):
    copies = out_ref.shape[0]
    for at, ref in enumerate((coords_ref, beside_ref)):
        for row in range(6):
            piece = ref[row // 2 : row // 2 + 1, cols(row % 2)]
            out_ref[:, 8 * at + row, :] = jnp.broadcast_to(piece, (copies, BLOCK))
        out_ref[:, 8 * at + 6 : 8 * at + 8, :] = jnp.zeros((copies, 2, BLOCK), F32)


def spread(coords, beside, copies):
    return pl.pallas_call(
        spread_kernel,
        out_shape=shape_of(copies, 16, BLOCK),
        compiler_params=params(),
        cost_estimate=cost(0.1),
        name="spread",
    )(coords, beside)


def lookup_kernel(order_ref, table_ref, out_ref):
    mine = lax.axis_index("row")
    side = lax.axis_index("leaf") & 1
    numbers = order_ref[...]
    owner = numbers >> 8
    leaf_of = owner >> 2
    count = table_ref.shape[0]
    far = (leaf_of & 1) ^ side
    key = (2 * far + ((numbers >> 7) & 1)) * count + (leaf_of >> 1)
    key = jnp.where((owner & 3) == mine, key, -1)
    shape = (4 * count, numbers.shape[1])
    chosen = (lax.broadcasted_iota(jnp.int32, shape, 0) == key).astype(F32)
    lane = lax.broadcasted_iota(jnp.int32, (BLOCK, numbers.shape[1]), 0) == (numbers & 127)
    out_ref[...] = jnp.zeros_like(out_ref)
    for part in range(3):
        rows = (2 * part, 2 * part + 1, 8 + 2 * part, 9 + 2 * part)
        piece = jnp.concatenate([table_ref[:, row, :] for row in rows], axis=0)
        found = full_dot(piece.T, chosen)
        out_ref[part : part + 1, :] = jnp.sum(jnp.where(lane, found, 0.0), axis=0, keepdims=True)


def lookup(order_row, table):
    return pl.pallas_call(
        lookup_kernel,
        out_shape=jax.ShapeDtypeStruct((8, order_row.shape[1]), F32),
        compiler_params=params(),
        cost_estimate=cost(1.5),
        name="lookup",
    )(order_row, table)


def pivot_inverse(pivot, largest, products, between):
    scale = 2.0 / (largest + 1.0)
    cheb = (largest + 1.0) / (largest - 1.0)
    residual = eye() - scale * pivot
    total = eye()
    for step in range(products):
        total = total + (three_dot(residual, total) if step else residual)
        doubled = jnp.minimum(2.0 * cheb * cheb - 1.0, 1e18)
        grow, drop = (doubled + 1.0) / doubled, 1.0 / doubled
        scale = scale * grow
        cheb = doubled
        if step + 1 < products:
            residual = grow * three_dot(residual, residual) - drop * eye()
        for piece in between[step::products]:
            piece()
    return scale * total


def turn(rhs_ref, turned_ref, at):
    core = lax.axis_index("row") & 1
    for level in range(turned_ref.shape[0] // HALF):
        turned = rhs_ref[at, cols(level)].T
        half = jnp.where(core == 0, turned[:HALF], turned[HALF:])
        turned_ref[level * HALF : (level + 1) * HALF, at] = half


def eliminate_any(mat_ref, rhs_ref, sol_ref, own_x_ref, turned_ref, held, right_ref, largest):
    blocks = mat_ref.shape[0] // BLOCK

    def place(block):
        return pl.ds(pl.multiple_of(block * BLOCK, BLOCK), BLOCK)

    def product(_, carry):
        scale, cheb = carry
        doubled = jnp.minimum(2.0 * cheb * cheb - 1.0, 1e18)
        grow = (doubled + 1.0) / doubled
        held[1] = held[1] + full_dot(held[0], held[1])
        held[0] = grow * full_dot(held[0], held[0]) - eye() / doubled
        return scale * grow, doubled

    def step(block, _):
        at = place(block)
        held[0] = eye() - 2.0 / (largest + 1.0) * mat_ref[at, at]
        held[1] = eye()
        scale = lax.fori_loop(
            0, MANY, product, (2.0 / (largest + 1.0), (largest + 1.0) / (largest - 1.0))
        )[0]
        held[1] = scale * held[1]
        solved = full_dot(held[1], rhs_ref[at, :])
        sol_ref[at, :] = solved
        right = full_dot(held[1], mat_ref[at, :])

        @pl.when(block == blocks - 2)
        def _():
            right_ref[...] = right[:, cols(blocks - 1)]

        def below(index, _):
            row = place(index)
            left = mat_ref[row, at]
            mat_ref[row, :] -= full_dot(left, right)
            rhs_ref[row, :] -= full_dot(left, solved)
            return 0

        lax.fori_loop(block + 1, blocks, below, 0)
        turn(rhs_ref, turned_ref, at)
        return 0

    lax.fori_loop(0, blocks, step, 0)
    last = sol_ref[cols(blocks - 1), :]
    own_x_ref[cols(1), :] = last
    own_x_ref[cols(0), :] = sol_ref[cols(blocks - 2), :] - full_dot(right_ref[...], last)


def eliminate(mat_ref, rhs_ref, sol_ref, own_x_ref, turned_ref, largest, between):
    blocks = mat_ref.shape[0] // BLOCK
    pivot = mat_ref[cols(0), cols(0)]
    right = None

    for block in range(blocks):
        inverse = pivot_inverse(pivot, largest[block], FEW, between)
        after = blocks - block - 1
        solved = three_dot(inverse, rhs_ref[cols(block), :])
        sol_ref[cols(block), :] = solved
        if after == 0:
            break
        right = three_dot(inverse, mat_ref[cols(block), cols(block + 1, after)])
        down = mat_ref[cols(block + 1, after), cols(block)]
        pivot = mat_ref[cols(block + 1), cols(block + 1)] - three_dot(
            down[:BLOCK], right[:, :BLOCK]
        )
        high, low = split(down)
        left = jnp.concatenate([high, high, low], axis=1)
        high, low = split(right)
        mat_right = jnp.concatenate([high, low, high], axis=0)
        high, low = split(solved)
        rhs_right = jnp.concatenate([high, low, high], axis=0)

        def piece(index, block=block, left=left, mat_right=mat_right, rhs_right=rhs_right):
            row = cols(block + 1 + index)
            part = left[cols(index)]
            mat_ref[row, cols(block + 1, blocks - block - 1)] -= half_dot(part, mat_right)
            rhs_ref[row, :] -= half_dot(part, rhs_right)

        between = [functools.partial(piece, index) for index in range(after)]
        between.append(functools.partial(turn, rhs_ref, turned_ref, cols(block)))
    turn(rhs_ref, turned_ref, cols(blocks - 1))
    own_x_ref[cols(1), :] = solved
    own_x_ref[cols(0), :] = sol_ref[cols(blocks - 2), :] - three_dot(right, solved)


def leaf_kernel(
    own_ref, core_ref, chip_ref, far_ref, *refs, levels, scales
):
    basis_refs, target_refs = refs[:4], refs[4:8]
    first_ref, next_ref, soon_ref, rest_ref, own_x_ref = refs[8:13]
    mat_ref, rhs_ref, sol_ref, turned_ref, held_ref, right_ref, points_ref = refs[13:20]
    size = mat_ref.shape[0]
    blocks = size // BLOCK
    piece = size // 4
    width = rhs_ref.shape[1]
    pieces = []
    for spot in range(4):
        total = own_ref[:, spot * piece : (spot + 1) * piece]
        for mask, ref in ((1, core_ref), (2, chip_ref), (3, far_ref)):
            other = spot ^ mask
            total = total + ref[:, other * piece : (other + 1) * piece]
        pieces.append(total)
    points = jnp.concatenate(pieces, axis=1)
    for spot in range(4):
        rows = slice(spot * piece, (spot + 1) * piece)
        for level in range(levels):
            rhs_ref[rows, cols(level)] = basis_refs[spot][level] * scales[level]
        rhs_ref[rows, cols(levels)] = target_refs[spot][...]
    def kernel_rows(turned, at):
        squared = jnp.zeros((BLOCK, at.stop - at.start), F32)
        for part in range(3):
            offset = turned[:, part : part + 1] - points[part : part + 1, at]
            squared = squared + offset * offset
        return jnp.exp(squared * (-0.5 / (LENGTH_SCALE * LENGTH_SCALE)))

    largest, turned_points = [], []
    for block in range(blocks):
        turned_points.append(points[:, cols(block)].T)
        points_ref[cols(block), :] = turned_points[block]
        value = kernel_rows(turned_points[block], cols(block)) + NOISE_VAR * eye()
        mat_ref[cols(block), cols(block)] = value
        sums = jnp.sum(value, axis=0, keepdims=True)
        largest.append(jnp.max(sums, axis=1, keepdims=True) + 0.01)

    def build(block):
        for at in (slice(0, block * BLOCK), slice((block + 1) * BLOCK, size)):
            if at.stop > at.start:
                mat_ref[cols(block), at] = kernel_rows(turned_points[block], at)

    def build_any(block, _):
        at = pl.ds(pl.multiple_of(block * BLOCK, BLOCK), BLOCK)
        diagonal = mat_ref[at, at]
        mat_ref[at, :] = kernel_rows(points_ref[at, :], slice(0, size))
        mat_ref[at, at] = diagonal
        return 0

    bound = largest[0]
    for value in largest[1:]:
        bound = jnp.maximum(bound, value)
    small = jnp.max(bound) < FEW_LIMIT
    rows = [functools.partial(build, block) for block in range(blocks)]

    @pl.when(small)
    def _():
        eliminate(mat_ref, rhs_ref, sol_ref, own_x_ref, turned_ref, largest, rows)

    @pl.when(jnp.logical_not(small))
    def _():
        lax.fori_loop(0, blocks, build_any, 0)
        eliminate_any(
            mat_ref, rhs_ref, sol_ref, own_x_ref, turned_ref, held_ref, right_ref, bound
        )

    high, low = split(sol_ref[...])
    left_high, left_low = split(turned_ref[...])
    chunks = []
    for at in range(0, levels + 1, 2):
        rows = HALF * min(levels, at + 2)
        here = cols(at, min(2, levels + 1 - at))
        both = half_dot(
            jnp.concatenate([left_high[:rows], left_low[:rows]], axis=0), high[:, here]
        )
        chunks.append(both[:rows] + (both[rows:] + half_dot(left_high[:rows], low[:, here])))

    start = 0
    for level in range(levels):
        mine = slice(level * HALF, (level + 1) * HALF)
        value = jnp.concatenate(
            [chunks[level // 2][mine, (level % 2) * BLOCK :]]
            + [chunk[mine] for chunk in chunks[level // 2 + 1 :]],
            axis=1,
        )
        if level == 0:
            first_ref[...] = value
        elif level == 1:
            next_ref[...] = value
        elif level == 2:
            soon_ref[...] = value
        else:
            rest_ref[:, start : start + value.shape[1]] = value
            start += value.shape[1]


def rest_width(level, levels):
    return sum((levels + 1 - row) * BLOCK for row in range(level + 3, levels))


def shape_of(*shape):
    return jax.ShapeDtypeStruct(shape, F32)


def leaf(parts, bases, targets, scales):
    levels = len(scales)
    size = parts[0].shape[1]
    width = (levels + 1) * BLOCK
    return pl.pallas_call(
        functools.partial(leaf_kernel, levels=levels, scales=scales),
        out_shape=[
            shape_of(HALF, width),
            shape_of(HALF, width - BLOCK),
            shape_of(HALF, width - 2 * BLOCK),
            shape_of(HALF, rest_width(0, levels)),
            shape_of(2 * BLOCK, width),
        ],
        scratch_shapes=[
            pltpu.VMEM((size, size), F32),
            pltpu.VMEM((size, width), F32),
            pltpu.VMEM((size, width), F32),
            pltpu.VMEM((levels * HALF, size), F32),
            pltpu.VMEM((2, BLOCK, BLOCK), F32),
            pltpu.VMEM((BLOCK, BLOCK), F32),
            pltpu.VMEM((size, 8), F32),
        ],
        compiler_params=params(),
        cost_estimate=cost(30),
        name="leaf",
    )(*parts, *bases, *targets)


def whole(target_ref, mine_ref, other_ref):
    core = lax.axis_index("row") & 1
    target_ref[pl.ds(pl.multiple_of(core * HALF, HALF), HALF), :] = mine_ref[...]
    target_ref[pl.ds(pl.multiple_of((1 - core) * HALF, HALF), HALF), :] = other_ref[...]


def coefficients(own_ref, sib_ref, held):
    own_gram, sib_gram = own_ref[:, :BLOCK], sib_ref[:, :BLOCK]
    own_proj, sib_proj = own_ref[:, BLOCK:], sib_ref[:, BLOCK:]
    power = full_dot(own_gram, sib_gram)
    residual = own_proj - three_dot(own_gram, sib_proj)
    total = eye() + power
    power = full_dot(power, power)
    total = total + full_dot(power, total)
    power = full_dot(power, power)

    def norm(value):
        return jnp.max(jnp.sum(jnp.abs(value), axis=0, keepdims=True))

    held[0], held[1] = power, total + full_dot(power, total)

    def more(carry):
        return jnp.logical_and(carry[0] * carry[0] > ROUNDING, carry[1] < 40)

    def once(carry):
        power = full_dot(held[0], held[0])
        held[0] = power
        held[1] += full_dot(power, held[1])
        return norm(power), carry[1] + 1

    lax.while_loop(more, once, (norm(power), 0))
    sib_z = three_dot(held[1], residual)
    return sib_proj - three_dot(sib_gram, sib_z), sib_z


def level_kernel(*refs):
    own_mine_ref, own_other_ref, mine_ref, other_ref = refs[:4]
    own_ref, sib_ref, own_z_ref, sib_z_ref, held_ref = refs[4:]
    whole(own_ref, own_mine_ref, own_other_ref)
    whole(sib_ref, mine_ref, other_ref)
    own_z_ref[...], sib_z_ref[...] = coefficients(own_ref, sib_ref, held_ref)


def level_step(own_mine, own_other, mine, other):
    width = mine.shape[1]
    return pl.pallas_call(
        level_kernel,
        out_shape=[shape_of(BLOCK, width)] * 2 + [shape_of(BLOCK, width - BLOCK)] * 2,
        scratch_shapes=[pltpu.VMEM((2, BLOCK, BLOCK), F32)],
        compiler_params=params(),
        cost_estimate=cost(0.2),
        name="level",
    )(own_mine, own_other, mine, other)


def half_turned(own_ref, sib_ref, at):
    core = lax.axis_index("row") & 1
    turned = jnp.concatenate([own_ref[:, at].T, sib_ref[:, at].T], axis=1)
    return jnp.where(core == 0, turned[:HALF], turned[HALF:])


def parent_rows(refs, rest_ref, sib_rest_ref, rows, level, levels):
    own_ref, sib_ref, own_z_ref, sib_z_ref = refs
    both_z = jnp.concatenate([own_z_ref[...], sib_z_ref[...]], axis=0)
    start = 0
    for row in rows:
        span = (levels + 1 - row) * BLOCK
        here = slice(start, start + span)
        left = half_turned(own_ref, sib_ref, cols(row - level))
        yield (rest_ref[:, here] + sib_rest_ref[:, here]) - three_dot(
            left, both_z[:, (row - level - 1) * BLOCK :]
        )
        start += span


def row_kernel(*refs, row, level, levels, with_current):
    sums = parent_rows(refs[:4], refs[4], refs[5], [row], level, levels)
    if with_current:
        x_ref, out_ref, x_out_ref = refs[6:]
        x_out_ref[...] = x_ref[:, BLOCK:] - three_dot(x_ref[:, :BLOCK], refs[2][...])
    else:
        out_ref = refs[6]
    out_ref[...] = next(sums)


def row_step(whole_rows, mine, sib, row, level, levels, current=None):
    out_shape = [shape_of(*mine.shape)]
    operands = [*whole_rows, mine, sib]
    if current is not None:
        operands.append(current)
        out_shape.append(shape_of(current.shape[0], current.shape[1] - BLOCK))
    return pl.pallas_call(
        functools.partial(
            row_kernel, row=row, level=level, levels=levels, with_current=current is not None
        ),
        out_shape=out_shape,
        compiler_params=params(),
        cost_estimate=cost(0.1),
        name="row",
    )(*operands)


def rest_kernel(*refs, level, levels):
    x_ref, rest_ref, sib_rest_ref, x_out_ref, soon_ref = refs[4:9]
    rows = range(level + 3, levels)
    start = 0
    for row, value in zip(rows, parent_rows(refs[:4], rest_ref, sib_rest_ref, rows, level, levels)):
        if row == level + 3 or level + 5 == levels:
            at = 0 if row == level + 3 else soon_ref.shape[1] - value.shape[1]
            soon_ref[:, at : at + value.shape[1]] = value
        else:
            refs[9][:, start : start + value.shape[1]] = value
            start += value.shape[1]
    x_out_ref[...] = x_ref[:, BLOCK:] - three_dot(x_ref[:, :BLOCK], refs[2][...])


def rest_step(whole_rows, current, rest, sib_rest, level, levels):
    out_shape = [
        shape_of(current.shape[0], current.shape[1] - BLOCK),
        shape_of(HALF, (levels - level - 2) * BLOCK),
    ]
    after = rest_width(level + 1, levels)
    if level + 5 == levels:
        out_shape[1] = shape_of(HALF, out_shape[1].shape[1] + after)
    else:
        out_shape.append(shape_of(HALF, after))
    return pl.pallas_call(
        functools.partial(rest_kernel, level=level, levels=levels),
        out_shape=out_shape,
        compiler_params=params(),
        cost_estimate=cost(0.2),
        name="rest",
    )(*whole_rows, current, rest, sib_rest)


def pair_kernel(*refs, level, levels):
    x_ref, x_out_ref = refs[6], refs[9]
    values = parent_rows(refs[:4], refs[4], refs[5], range(level + 2, levels), level, levels)
    for out_ref, value in zip(refs[7:9], values):
        out_ref[...] = value
    x_out_ref[...] = x_ref[:, BLOCK:] - three_dot(x_ref[:, :BLOCK], refs[2][...])


def pair_step(whole_rows, mine, sib, current, level, levels):
    return pl.pallas_call(
        functools.partial(pair_kernel, level=level, levels=levels),
        out_shape=[
            shape_of(HALF, (levels - level - 1) * BLOCK),
            shape_of(HALF, (levels - level - 2) * BLOCK),
            shape_of(current.shape[0], current.shape[1] - BLOCK),
        ],
        compiler_params=params(),
        cost_estimate=cost(0.1),
        name="pair",
    )(*whole_rows, mine, sib, current)


def final_kernel(*refs):
    own_mine_ref, own_other_ref, mine_ref, other_ref, x_ref, before_z_ref, out_ref = refs[:7]
    own_ref, sib_ref, held_ref = refs[7:]
    whole(own_ref, own_mine_ref, own_other_ref)
    whole(sib_ref, mine_ref, other_ref)
    current = x_ref[:, BLOCK:] - three_dot(x_ref[:, :BLOCK], before_z_ref[...])
    own_z, _ = coefficients(own_ref, sib_ref, held_ref)
    out_ref[...] = current[:, BLOCK:] - three_dot(current[:, :BLOCK], own_z)


def final_step(own_mine, own_other, mine, other, current, before_z):
    whole_row = pltpu.VMEM((BLOCK, mine.shape[1]), F32)
    return pl.pallas_call(
        final_kernel,
        out_shape=shape_of(current.shape[0], BLOCK),
        scratch_shapes=[whole_row, whole_row, pltpu.VMEM((2, BLOCK, BLOCK), F32)],
        compiler_params=params(),
        cost_estimate=cost(0.2),
        name="final",
    )(own_mine, own_other, mine, other, current, before_z)


PARTNERS = (4 | 2, 8, 16 | 8, 32, 64, 128 | 64 | 32)


def on_device(coords, order, targets, bases):
    levels = bases.shape[0]
    rows = targets.shape[0]
    leaf_size = rows * lax.axis_size("row")
    scales = tuple(float((leaf_size * 2**level) ** (-0.5)) for level in range(levels))
    orders = [order] + [swap(order, mask) for mask in (1, 2, 3)]
    beside = swap(coords, 4)
    half = lax.axis_size("leaf") // 2
    groups = [[2 * index + side for index in range(half)] for side in range(2)]
    beside, sent_bases, sent_targets, *orders = lax.optimization_barrier(
        (beside, bases, targets, *orders)
    )
    chip_bases, chip_targets = swap(sent_bases, 2), swap(sent_targets, 2)
    table = lax.all_to_all(
        spread(coords, beside, half), "leaf", 0, 0, axis_index_groups=groups, tiled=True
    )
    chip_bases, chip_targets, _ = lax.optimization_barrier((chip_bases, chip_targets, table))
    order_row = jnp.concatenate(orders[::-1]).reshape(1, leaf_size)
    part = lookup(order_row, table)
    parts = [part] + [swap(part, mask) for mask in (1, 2, 3)]
    all_bases = [swap(chip_bases, 1), chip_bases, swap(bases, 1), bases]
    all_targets = [swap(chip_targets, 1), chip_targets, swap(targets, 1), targets]
    own, coming, soon, rest, current = leaf(parts, all_bases, all_targets, scales)
    waiting = None
    for level in range(levels):
        mask = PARTNERS[level]
        mine = swap(own, mask)
        own_other = swap(own, 1)
        if level == 0:
            sib_coming = swap(coming, mask)
            mine, sib_coming = lax.optimization_barrier((mine, sib_coming))
        other = swap(mine, 1)
        if level + 1 == levels:
            return final_step(own, own_other, mine, other, current, own_z)
        if level:
            coming, _ = lax.optimization_barrier((coming, own_other))
            sib_coming = swap(coming, mask)
        whole_rows = level_step(own, own_other, mine, other)
        own_z = whole_rows[2]
        if waiting is not None:
            sib_rest, _ = lax.optimization_barrier((sib_rest, own_z))
            new = rest_step(waiting, current, rest, sib_rest, level - 1, levels)
            current, soon = new[:2]
            rest = new[2] if len(new) > 2 else None
            waiting = None
        if level + 2 < levels:
            soon, _ = lax.optimization_barrier((soon, mine))
            sib_soon = swap(soon, mask)
        if level + 4 < levels:
            rest, _ = lax.optimization_barrier((rest, own_z))
            sib_rest = swap(rest, mask)
            waiting = whole_rows
        own = row_step(whole_rows, coming, sib_coming, level + 1, level, levels)[0]
        if level + 2 < levels:
            sib_soon, _ = lax.optimization_barrier((sib_soon, own))
            if level + 4 == levels:
                coming, soon, current = pair_step(
                    whole_rows, soon, sib_soon, current, level, levels
                )
                continue
            with_current = None if waiting is not None else current
            new = row_step(whole_rows, soon, sib_soon, level + 2, level, levels, with_current)
            coming = new[0]
            if waiting is None:
                current = new[1]


def solution(mesh):
    return jax.shard_map(
        on_device,
        mesh=mesh,
        in_specs=(
            P(None, AXES),
            P(AXES),
            P(AXES, None),
            P(None, AXES, None),
        ),
        out_specs=P(AXES, None),
        check_vma=False,
    )
```
